512 devices in a mesh: dp: 32 (over z, y_hi), fsdp: 16 (over x, y_lo, core).
Axes of the slice: x: 4, y: 4 (y_hi: 2, y_lo: 2; y = y_hi * 2 + y_lo), z: 16, core: 2. Of those that a mesh axis runs over, the one named last changes fastest.
Arguments:
- hidden: bfloat16 [65536, 8192], P(('dp', 'fsdp')), may hold values from -6 to 6
- target: bfloat16 [65536, 512], P(('dp', 'fsdp')), may hold values from -6 to 6
- base_weight: bfloat16 [8192, 512], P('fsdp'), may hold values from -0.0625 to 0.0625
- v_factor: float32 [8192, 128], P('fsdp'), may hold values from -0.0625 to 0.0625
- u_factor: float32 [512, 128], replicated, may hold values from -0.25 to 0.25
- sigma: float32 [128], replicated, may hold values from 0.5 to 4
- bits: int32 [128], replicated, may hold values from 2 to 8, as said below
- v_exps: int32 [128], replicated, may hold values from 6 to 9
- u_exps: int32 [128], replicated, may hold values from 4 to 7
Outputs:
- grad_v: float32 [8192, 128], P('fsdp')
- grad_u: float32 [512, 128], replicated
The draws below stay inside these ranges and needn't reach their ends.
Inputs may be any that keep to these rules, and one draw needn't show every extreme that they name: bits holds 8 for the first few singular vectors, then 3, then 2; it never rises along the vectors and all three widths occur.
All inputs are finite; a program needn't handle non-finite values.
Results may differ from the reference program's by a relative error of at most 0.003.
Values may be sent and summed in bfloat16 or wider, within the bound.
No kernel may reach another device: no remote copies, remote signals or barrier semaphores. Data moves between devices by JAX's collectives and lax.ppermute only.
A program may use at most 64 MiB of HBM per device.

```python
import math
import jax
import jax.numpy as jnp

D = 8192
KVW = 512
R = 128
TOKENS = 65536


def draw_bits(key, part):
    key = jax.random.fold_in(key, 11)
    first_key, second_key = jax.random.split(key)
    first = jax.random.randint(first_key, (), R // 16, R // 8 + 1)
    second = first + jax.random.randint(second_key, (), R // 4, R // 2 + 1)
    position = jnp.arange(R)
    return jnp.where(position < first, 8, jnp.where(position < second, 3, 2)).astype(jnp.int32)


def set_ends(values, key, least, high):
    shape = values.shape
    index_at = [jax.random.randint(jax.random.fold_in(key, axis), (), 0, shape[axis]) for axis in range(len(shape))]
    values = values.at[tuple(index_at)].set(least)
    longest = shape.index(max(shape))
    index_at[longest] = (index_at[longest] + 1) % shape[longest]
    return values.at[tuple(index_at)].set(high)


def shard_levels(rng, extent, cuts, low, top_value):
    def one(axis_at, blocks):
        steps = jax.random.uniform(jax.random.fold_in(jax.random.fold_in(rng, 6), axis_at), (blocks,), jnp.float32, low / len(cuts), top_value / len(cuts))
        return jnp.repeat(jnp.exp(steps), extent[axis_at] // blocks).reshape((-1,) + (1,) * (len(extent) - axis_at - 1))

    gain = one(*cuts[0])
    for cut in cuts[1:]:
        gain = gain * one(*cut)
    return gain


def scatter_about(key, extent, width, limit, cuts=(), dtype=jnp.bfloat16):
    level = shard_levels(key, extent, cuts, -0.22, 0.18) if cuts else 1.0
    array = jax.random.normal(key, extent, jnp.float32) * width * level
    return jnp.minimum(jnp.maximum(array, -limit), limit).astype(dtype)


def setup_inputs(seed: int = 0) -> dict:
    key_list = jax.random.split(jax.random.key(seed), 10)
    return {
        "hidden": scatter_about(key_list[0], (TOKENS, D), 1.0, 6.0, ((0, 512),)),
        "target": scatter_about(key_list[1], (TOKENS, KVW), 1.0, 6.0, ((0, 512),)),
        "base_weight": scatter_about(key_list[2], (D, KVW), D ** -0.5, 0.0625, ((0, 16),)),
        "v_factor": scatter_about(key_list[3], (D, R), D ** -0.5, 0.0625, ((0, 16),), jnp.float32),
        "u_factor": scatter_about(key_list[4], (KVW, R), KVW ** -0.5, 0.25, (), jnp.float32),
        "sigma": jnp.clip(jnp.exp(jax.random.uniform(key_list[5], (R,), jnp.float32, math.log(0.5), math.log(4.0))), 0.5, 4.0),
        "bits": draw_bits(jax.random.fold_in(key_list[9], 71), 0),
        "v_exps": set_ends(jax.random.randint(key_list[7], (R,), 6, 10), jax.random.fold_in(key_list[7], 1), 6, 9).astype(jnp.int32),
        "u_exps": set_ends(jax.random.randint(key_list[8], (R,), 4, 8), jax.random.fold_in(key_list[8], 1), 4, 7).astype(jnp.int32),
    }


def fake_quantize(factor, bits, scale_exps):
    step = jnp.exp2(-scale_exps.astype(jnp.float32))
    upper = jnp.exp2(bits.astype(jnp.float32) - 1.0)
    ratio = factor / step
    smooth = ratio - jnp.sin(2.0 * math.pi * ratio) / (2.0 * math.pi)
    return step * jnp.clip(smooth, -upper, upper - 1.0)

def reference(hidden, target, base_weight, v_factor, u_factor, sigma, bits, v_exps, u_exps):
    v_quant = fake_quantize(v_factor, bits, v_exps).astype(jnp.bfloat16)
    u_quant = fake_quantize(u_factor, bits, u_exps).astype(jnp.bfloat16)
    base_out = jnp.dot(hidden, base_weight, preferred_element_type=jnp.float32)
    low_rank = jnp.dot(hidden, v_quant, preferred_element_type=jnp.float32)
    scaled = (low_rank * sigma).astype(jnp.bfloat16)
    residual = base_out + jnp.dot(scaled, u_quant.T, preferred_element_type=jnp.float32) - target.astype(jnp.float32)
    out_grad = (residual * (1.0 / math.sqrt(hidden.shape[0]))).astype(jnp.bfloat16)
    grad_u = jnp.dot(out_grad.T, scaled, preferred_element_type=jnp.float32)
    rank_grad = (jnp.dot(out_grad, u_quant, preferred_element_type=jnp.float32) * sigma).astype(jnp.bfloat16)
    grad_v = jnp.dot(hidden.T, rank_grad, preferred_element_type=jnp.float32)
    return (grad_v, grad_u)
```

```python
import math

import jax
import jax.numpy as jnp
from jax import lax
from jax.sharding import PartitionSpec as P


def fake_quantize(factor, bits, scale_exps):
    step = jnp.exp2(-scale_exps.astype(jnp.float32))
    upper = jnp.exp2(bits.astype(jnp.float32) - 1.0)
    ratio = factor / step
    smooth = ratio - jnp.sin(2.0 * math.pi * ratio) / (2.0 * math.pi)
    return step * jnp.clip(smooth, -upper, upper - 1.0)


def scatter_sum(parts, axis):
    return jnp.sum(lax.all_to_all(parts, axis, 0, 0, tiled=True), axis=0)


def spread(rows, axis):
    n = lax.axis_size(axis)
    return lax.all_to_all(jnp.broadcast_to(rows, (n, *rows.shape)), axis, 0, 0, tiled=True)


def shards(hidden, target, base_weight, v_factor, u_factor, sigma, bits, v_exps, u_exps):
    n_fsdp, n_dp = lax.axis_size("fsdp"), lax.axis_size("dp")
    v_quant = fake_quantize(v_factor, bits, v_exps).astype(jnp.bfloat16)
    u_quant = fake_quantize(u_factor, bits, u_exps).astype(jnp.bfloat16)
    tok_rows = hidden.shape[0]
    kvw, rank = u_factor.shape

    both = lax.all_gather(jnp.concatenate([base_weight, v_quant], axis=1), "fsdp", axis=0, tiled=True)
    out = jnp.dot(hidden, both, preferred_element_type=jnp.float32)
    base_out, low_rank = out[:, :kvw], out[:, kvw:]
    scaled = (low_rank * sigma).astype(jnp.bfloat16)
    residual = (
        base_out
        + jnp.dot(scaled, u_quant.T, preferred_element_type=jnp.float32)
        - target.astype(jnp.float32)
    )
    tokens_all = tok_rows * n_dp * n_fsdp
    out_grad = (residual * (1.0 / math.sqrt(tokens_all))).astype(jnp.bfloat16)
    grad_u_part = jnp.einsum("tk,tr->kr", out_grad, scaled, preferred_element_type=jnp.float32)
    rank_grad = (jnp.dot(out_grad, u_quant, preferred_element_type=jnp.float32) * sigma).astype(
        jnp.bfloat16
    )
    grad_v_part = jnp.einsum("td,tr->dr", hidden, rank_grad, preferred_element_type=jnp.float32)

    parts = jnp.concatenate(
        [grad_v_part.reshape(n_fsdp, -1, rank), grad_u_part.reshape(n_fsdp, -1, rank)], axis=1
    )
    mine = scatter_sum(parts, "fsdp")
    rows_v = v_factor.shape[0]
    parts = jnp.concatenate(
        [mine[:rows_v].reshape(n_dp, -1, rank), mine[rows_v:].reshape(n_dp, -1, rank)], axis=1
    )
    mine = scatter_sum(parts, "dp")
    whole = spread(mine, "dp")
    per_v = rows_v // n_dp
    grad_v = whole[:, :per_v].reshape(rows_v, rank)
    grad_u = spread(whole[:, per_v:].reshape(-1, rank), "fsdp").reshape(kvw, rank)
    return (grad_v, grad_u)


def solution(mesh):
    in_specs = (
        P(("dp", "fsdp"), None),
        P(("dp", "fsdp"), None),
        P("fsdp", None),
        P("fsdp", None),
        P(),
        P(),
        P(),
        P(),
        P(),
    )
    out_specs = (P("fsdp", None), P())
    return jax.shard_map(shards, mesh=mesh, in_specs=in_specs, out_specs=out_specs, check_vma=False)
```

```python
import math

import jax
import jax.numpy as jnp
from jax import lax
from jax.sharding import Mesh, PartitionSpec as P

AXES = {"z": 16, "yh": 2, "x": 4, "yl": 2, "core": 2}
DP, FSDP, CHIPS = ("z", "yh"), ("x", "yl", "core"), ("x", "yl")


def fake_quantize(factor, bits, scale_exps):
    step = jnp.exp2(-scale_exps.astype(jnp.float32))
    upper = jnp.exp2(bits.astype(jnp.float32) - 1.0)
    ratio = factor / step
    smooth = ratio - jnp.sin(2.0 * math.pi * ratio) / (2.0 * math.pi)
    return step * jnp.clip(smooth, -upper, upper - 1.0)


def exchange(parts, axes):
    return lax.all_to_all(parts, axes, 0, 0, tiled=True)


def spread(rows, axes):
    return exchange(jnp.broadcast_to(rows, (lax.axis_size(axes), *rows.shape)), axes)


def shards(hidden, target, base_weight, v_factor, u_factor, sigma, bits, v_exps, u_exps):
    n_z, n_yh, n_chips = lax.axis_size("z"), lax.axis_size("yh"), lax.axis_size(CHIPS)
    tok, _ = hidden.shape
    kvw, rank = u_factor.shape
    rows = v_factor.shape[0]

    v_quant = fake_quantize(v_factor, bits, v_exps).astype(jnp.bfloat16)
    weights = lax.all_gather(
        jnp.concatenate([base_weight, v_quant], axis=1), CHIPS, axis=0, tiled=True
    )
    by_core = hidden.reshape(tok, n_chips, 2, rows).transpose(2, 0, 1, 3).reshape(2, tok, -1)
    pair = exchange(by_core, "core").reshape(2 * tok, -1)
    u_quant = fake_quantize(u_factor, bits, u_exps).astype(jnp.bfloat16)

    part = jnp.dot(pair, weights, preferred_element_type=jnp.float32)
    out = jnp.sum(exchange(part.reshape(2, tok, -1), "core"), axis=0)
    base_out, low_rank = out[:, :kvw], out[:, kvw:]
    scaled = (low_rank * sigma).astype(jnp.bfloat16)
    residual = (
        base_out
        + jnp.dot(scaled, u_quant.T, preferred_element_type=jnp.float32)
        - target.astype(jnp.float32)
    )
    tokens_all = tok * n_z * n_yh * n_chips * 2
    out_grad = (residual * (1.0 / math.sqrt(tokens_all))).astype(jnp.bfloat16)
    rank_grad = jnp.dot(out_grad, u_quant, preferred_element_type=jnp.float32) * sigma
    rank_pair = spread(rank_grad.astype(jnp.bfloat16), "core").reshape(2 * tok, rank)
    grad_u_part = jnp.einsum("tk,tr->kr", out_grad, scaled, preferred_element_type=jnp.float32)
    u_half = grad_u_part.reshape(n_chips, 2, -1, rank).transpose(1, 0, 2, 3)
    u_half = jnp.sum(exchange(u_half, "core"), axis=0)
    grad_v_part = jnp.einsum("td,tr->dr", pair, rank_pair, preferred_element_type=jnp.float32)

    half = rows // n_yh
    u_parts = jnp.broadcast_to(u_half[:, None], (n_chips, n_yh, *u_half.shape[1:]))
    parts = jnp.concatenate(
        [grad_v_part.reshape(n_chips * n_yh, half, rank), u_parts.reshape(n_chips * n_yh, -1, rank)],
        axis=1,
    )
    mine = jnp.sum(exchange(parts, (*CHIPS, "yh")), axis=0)
    mine = jnp.concatenate(
        [mine[:half].reshape(n_z, -1, rank), mine[half:].reshape(n_z, -1, rank)], axis=1
    )
    mine = jnp.sum(exchange(mine, "z"), axis=0)
    whole = spread(mine, "z")
    per_z = half // n_z
    v_mine = whole[:, :per_z].reshape(-1, rank)
    v_other = lax.ppermute(v_mine, "yh", [(0, 1), (1, 0)])
    low = lax.axis_index("yh") == 0
    grad_v = jnp.concatenate(
        [jnp.where(low, v_mine, v_other), jnp.where(low, v_other, v_mine)], axis=0
    )
    grad_u = spread(whole[:, per_z:].reshape(-1, rank), FSDP).reshape(kvw, rank)
    return (grad_v, grad_u)


def solution(mesh):
    fine = Mesh(mesh.devices.reshape(tuple(AXES.values())), tuple(AXES))
    in_specs = (
        P((*DP, *FSDP), None),
        P((*DP, *FSDP), None),
        P(FSDP, None),
        P(FSDP, None),
        P(),
        P(),
        P(),
        P(),
        P(),
    )
    out_specs = (P(FSDP, None), P())
    return jax.shard_map(shards, mesh=fine, in_specs=in_specs, out_specs=out_specs, check_vma=False)
```

```python
import math

import jax
import jax.numpy as jnp
from jax import lax
from jax.sharding import Mesh, PartitionSpec as P

AXES = {"z": 16, "yh": 2, "x": 4, "yl": 2, "core": 2}
DP, FSDP, NEAR = ("z", "yh"), ("x", "yl", "core"), ("yl", "core")


def fake_quantize(factor, bits, scale_exps):
    step = jnp.exp2(-scale_exps.astype(jnp.float32))
    upper = jnp.exp2(bits.astype(jnp.float32) - 1.0)
    ratio = factor / step
    smooth = ratio - jnp.sin(2.0 * math.pi * ratio) / (2.0 * math.pi)
    return step * jnp.clip(smooth, -upper, upper - 1.0)


def exchange(parts, axes):
    return lax.all_to_all(parts, axes, 0, 0, tiled=True)


def spread(rows, axes):
    return exchange(jnp.broadcast_to(rows, (lax.axis_size(axes), *rows.shape)), axes)


def shards(hidden, target, base_weight, v_factor, u_factor, sigma, bits, v_exps, u_exps):
    n_x, n_z, n_yh = lax.axis_size("x"), lax.axis_size("z"), lax.axis_size("yh")
    n_near = lax.axis_size(NEAR)
    tok, _ = hidden.shape
    kvw, rank = u_factor.shape
    rows = v_factor.shape[0]
    me = lax.axis_index(NEAR)

    v_quant = fake_quantize(v_factor, bits, v_exps).astype(jnp.bfloat16)
    weights = [jnp.concatenate([base_weight, v_quant], axis=1)]
    for k in range(1, n_near):
        weights.append(lax.ppermute(weights[0], NEAR, [(j, j ^ k) for j in range(n_near)]))
    wide = n_near * rows
    columns = jnp.stack([hidden[:, i * wide : (i + 1) * wide] for i in range(n_x)])
    tokens = exchange(columns, "x").reshape(n_x * tok, wide)
    u_quant = fake_quantize(u_factor, bits, u_exps).astype(jnp.bfloat16)

    part = sum(
        jnp.dot(
            lax.dynamic_slice_in_dim(tokens, (me ^ k) * rows, rows, 1),
            weights[k],
            preferred_element_type=jnp.float32,
        )
        for k in range(n_near)
    )
    out = jnp.sum(exchange(part.reshape(n_x, tok, -1), "x"), axis=0)
    base_out, low_rank = out[:, :kvw], out[:, kvw:]
    scaled = (low_rank * sigma).astype(jnp.bfloat16)
    residual = (
        base_out
        + jnp.dot(scaled, u_quant.T, preferred_element_type=jnp.float32)
        - target.astype(jnp.float32)
    )
    tokens_all = tok * n_z * n_yh * n_x * n_near
    out_grad = (residual * (1.0 / math.sqrt(tokens_all))).astype(jnp.bfloat16)
    rank_grad = jnp.dot(out_grad, u_quant, preferred_element_type=jnp.float32) * sigma
    rank_all = spread(rank_grad.astype(jnp.bfloat16), "x").reshape(n_x * tok, rank)
    grad_u_part = jnp.einsum("tk,tr->kr", out_grad, scaled, preferred_element_type=jnp.float32)
    u_rows = jnp.sum(exchange(grad_u_part.reshape(n_x, -1, rank), "x"), axis=0)
    grad_v_part = jnp.einsum("td,tr->dr", tokens, rank_all, preferred_element_type=jnp.float32)

    half = rows // n_yh
    v_parts = grad_v_part.reshape(n_near * n_yh, half, rank)
    u_parts = u_rows.reshape(n_near, 1, -1, rank)
    u_parts = jnp.broadcast_to(u_parts, (n_near, n_yh, *u_parts.shape[2:]))
    parts = jnp.concatenate([v_parts, u_parts.reshape(n_near * n_yh, -1, rank)], axis=1)
    mine = jnp.sum(exchange(parts, (*NEAR, "yh")), axis=0)
    mine = jnp.concatenate(
        [mine[:half].reshape(n_z, -1, rank), mine[half:].reshape(n_z, -1, rank)], axis=1
    )
    mine = jnp.sum(exchange(mine, "z"), axis=0)
    whole = spread(mine, "z")
    per_z = half // n_z
    v_mine = whole[:, :per_z].reshape(-1, rank)
    v_other = lax.ppermute(v_mine, "yh", [(0, 1), (1, 0)])
    low = lax.axis_index("yh") == 0
    grad_v = jnp.concatenate(
        [jnp.where(low, v_mine, v_other), jnp.where(low, v_other, v_mine)], axis=0
    )
    grad_u = spread(whole[:, per_z:].reshape(-1, rank), FSDP).reshape(kvw, rank)
    return (grad_v, grad_u)


def solution(mesh):
    fine = Mesh(mesh.devices.reshape(tuple(AXES.values())), tuple(AXES))
    in_specs = (
        P((*DP, *FSDP), None),
        P((*DP, *FSDP), None),
        P(FSDP, None),
        P(FSDP, None),
        P(),
        P(),
        P(),
        P(),
        P(),
    )
    out_specs = (P(FSDP, None), P())
    return jax.shard_map(shards, mesh=fine, in_specs=in_specs, out_specs=out_specs, check_vma=False)
```

```python
import functools
import math

import jax
import jax.numpy as jnp
from jax import lax
from jax.experimental import pallas as pl
from jax.experimental.pallas import tpu as pltpu
from jax.sharding import Mesh, PartitionSpec as P

AXES = {"z": 16, "yh": 2, "x": 4, "yl": 2, "core": 2}
DP, FSDP, NEAR = ("z", "yh"), ("x", "yl", "core"), ("yl", "core")


def fake_quantize(factor, bits, scale_exps):
    step = jnp.exp2(-scale_exps.astype(jnp.float32))
    upper = jnp.exp2(bits.astype(jnp.float32) - 1.0)
    ratio = factor / step
    smooth = ratio - jnp.sin(2.0 * math.pi * ratio) / (2.0 * math.pi)
    return step * jnp.clip(smooth, -upper, upper - 1.0)


def exchange(parts, axes):
    return lax.all_to_all(parts, axes, 0, 0, tiled=True)


def spread(rows, axes):
    return exchange(jnp.broadcast_to(rows, (lax.axis_size(axes), *rows.shape)), axes)


IN_VMEM = pl.BlockSpec(memory_space=pltpu.VMEM)
IN_SMEM = pl.BlockSpec(memory_space=pltpu.SMEM)
PARAMS = pltpu.CompilerParams(vmem_limit_bytes=40 * 1024 * 1024)


def dot32(a, b, dims=((1,), (0,))):
    return lax.dot_general(a, b, (dims, ((), ())), preferred_element_type=jnp.float32)


def partial_kernel(order_ref, tokens_ref, *refs):
    *piece_refs, out_ref = refs
    n_x, tok, _ = out_ref.shape
    rows = piece_refs[0].shape[0]
    for i in range(n_x):
        total = None
        for k, piece in enumerate(piece_refs):
            start = pl.multiple_of(order_ref[k] * rows, rows)
            term = dot32(tokens_ref[i * tok : (i + 1) * tok, pl.ds(start, rows)], piece[...])
            total = term if total is None else total + term
        out_ref[i] = total


def middle_kernel(scale, parts_ref, target_ref, u_ref, sigma_ref, out_ref):
    n_x, tok, _ = parts_ref.shape
    kvw, rank = u_ref.shape
    out = parts_ref[0]
    for i in range(1, n_x):
        out = out + parts_ref[i]
    sigma = sigma_ref[...]
    u_quant = u_ref[...]
    scaled = (out[:, kvw:] * sigma).astype(jnp.bfloat16)
    residual = out[:, :kvw] + dot32(scaled, u_quant, ((1,), (1,))) - target_ref[...].astype(jnp.float32)
    out_grad = (residual * scale).astype(jnp.bfloat16)
    rank_grad = (dot32(out_grad, u_quant) * sigma).astype(jnp.bfloat16).astype(jnp.float32)
    each = kvw // n_x
    for i in range(n_x):
        out_ref[i, :tok] = rank_grad
        out_ref[i, tok:] = dot32(out_grad[:, i * each : (i + 1) * each], scaled, ((0,), (0,)))


def grads_kernel(tokens_ref, arrived_ref, out_ref):
    n_x, both, rank = arrived_ref.shape
    n_to, packed, _ = out_ref.shape
    tok = tokens_ref.shape[0] // n_x
    half = tokens_ref.shape[1] // n_to
    rank_all = jnp.concatenate([arrived_ref[i, :tok] for i in range(n_x)], axis=0)
    rank_all = rank_all.astype(jnp.bfloat16)
    u_rows = arrived_ref[0, tok:]
    for i in range(1, n_x):
        u_rows = u_rows + arrived_ref[i, tok:]
    u_rows = u_rows.astype(jnp.bfloat16)
    each = packed - half
    n_near = (both - tok) // each
    for i in range(n_to):
        v_rows = dot32(tokens_ref[:, i * half : (i + 1) * half], rank_all, ((0,), (0,)))
        out_ref[i, :half] = v_rows.astype(jnp.bfloat16)
        near = i * n_near // n_to
        out_ref[i, half:] = u_rows[near * each : (near + 1) * each]


def shards(hidden, target, base_weight, v_factor, u_factor, sigma, bits, v_exps, u_exps):
    n_x, n_z, n_yh = lax.axis_size("x"), lax.axis_size("z"), lax.axis_size("yh")
    n_near = lax.axis_size(NEAR)
    tok, _ = hidden.shape
    kvw, rank = u_factor.shape
    rows = v_factor.shape[0]
    me = lax.axis_index(NEAR)
    swap = [(0, 1), (1, 0)]

    v_quant = fake_quantize(v_factor, bits, v_exps).astype(jnp.bfloat16)
    own = jnp.concatenate([base_weight, v_quant], axis=1)
    across = lax.ppermute(own, "yl", swap)
    pieces = [own, lax.ppermute(own, "core", swap), across, lax.ppermute(across, "core", swap)]
    wide = n_near * rows
    columns = jnp.stack([hidden[:, i * wide : (i + 1) * wide] for i in range(n_x)])
    tokens = exchange(columns, "x").reshape(n_x * tok, wide)
    u_quant = fake_quantize(u_factor, bits, u_exps).astype(jnp.bfloat16)

    f32, order = jnp.float32, jnp.bitwise_xor(me, jnp.arange(n_near, dtype=jnp.int32))
    part = pl.pallas_call(
        partial_kernel,
        out_shape=jax.ShapeDtypeStruct((n_x, tok, kvw + rank), f32),
        in_specs=[IN_SMEM] + [IN_VMEM] * (1 + n_near),
        out_specs=IN_VMEM,
        compiler_params=PARAMS,
        name="partial_products",
    )(order, tokens, *pieces)
    scale = 1.0 / math.sqrt(tok * n_z * n_yh * n_x * n_near)
    ranks = pl.pallas_call(
        functools.partial(middle_kernel, scale),
        out_shape=jax.ShapeDtypeStruct((n_x, tok + kvw // n_x, rank), f32),
        in_specs=[IN_VMEM] * 4,
        out_specs=IN_VMEM,
        compiler_params=PARAMS,
        name="residual_and_grad_u",
    )(exchange(part, "x"), target, u_quant, sigma.reshape(1, rank))
    half = rows // n_yh
    parts = pl.pallas_call(
        grads_kernel,
        out_shape=jax.ShapeDtypeStruct((n_near * n_yh, half + kvw // (n_x * n_near), rank), jnp.bfloat16),
        in_specs=[IN_VMEM] * 2,
        out_specs=IN_VMEM,
        compiler_params=PARAMS,
        name="grad_v_packed",
    )(tokens, exchange(ranks, "x"))
    mine = jnp.sum(exchange(parts, (*NEAR, "yh")).astype(f32), axis=0)
    mine = jnp.concatenate(
        [mine[:half].reshape(n_z, -1, rank), mine[half:].reshape(n_z, -1, rank)], axis=1
    )
    mine = jnp.sum(exchange(mine, "z"), axis=0)
    whole = spread(mine, "z")
    per_z = half // n_z
    v_mine = whole[:, :per_z].reshape(-1, rank)
    v_other = lax.ppermute(v_mine, "yh", swap)
    low = lax.axis_index("yh") == 0
    grad_v = jnp.concatenate(
        [jnp.where(low, v_mine, v_other), jnp.where(low, v_other, v_mine)], axis=0
    )
    grad_u = spread(whole[:, per_z:].reshape(-1, rank), FSDP).reshape(kvw, rank)
    return (grad_v, grad_u)


def solution(mesh):
    fine = Mesh(mesh.devices.reshape(tuple(AXES.values())), tuple(AXES))
    in_specs = (
        P((*DP, *FSDP), None),
        P((*DP, *FSDP), None),
        P(FSDP, None),
        P(FSDP, None),
        P(),
        P(),
        P(),
        P(),
        P(),
    )
    out_specs = (P(FSDP, None), P())
    return jax.shard_map(shards, mesh=fine, in_specs=in_specs, out_specs=out_specs, check_vma=False)
```

```python
import functools
import math

import jax
import jax.numpy as jnp
from jax import lax
from jax.experimental import pallas as pl
from jax.experimental.pallas import tpu as pltpu
from jax.sharding import Mesh, PartitionSpec as P

AXES = {"z1": 4, "z0": 4, "yh": 2, "x": 4, "yl": 2, "core": 2}
DP, FSDP, NEAR = ("z1", "z0", "yh"), ("x", "yl", "core"), ("yl", "core")
CLOSE, FAR = (*NEAR, "yh", "z0"), ("z1", "yh")


def fake_quantize(factor, bits, scale_exps):
    step = jnp.exp2(-scale_exps.astype(jnp.float32))
    upper = jnp.exp2(bits.astype(jnp.float32) - 1.0)
    ratio = factor / step
    smooth = ratio - jnp.sin(2.0 * math.pi * ratio) / (2.0 * math.pi)
    return step * jnp.clip(smooth, -upper, upper - 1.0)


def exchange(parts, axes):
    return lax.all_to_all(parts, axes, 0, 0, tiled=True)


IN_VMEM = pl.BlockSpec(memory_space=pltpu.VMEM)
IN_SMEM = pl.BlockSpec(memory_space=pltpu.SMEM)
PARAMS = pltpu.CompilerParams(vmem_limit_bytes=40 * 1024 * 1024)


def dot32(a, b, dims=((1,), (0,))):
    return lax.dot_general(a, b, (dims, ((), ())), preferred_element_type=jnp.float32)


def partial_kernel(order_ref, tokens_ref, *refs):
    *piece_refs, out_ref = refs
    n_x, tok, _ = out_ref.shape
    rows = piece_refs[0].shape[0]
    for i in range(n_x):
        total = None
        for k, piece in enumerate(piece_refs):
            start = pl.multiple_of(order_ref[k] * rows, rows)
            term = dot32(tokens_ref[i * tok : (i + 1) * tok, pl.ds(start, rows)], piece[...])
            total = term if total is None else total + term
        out_ref[i] = total


def middle_kernel(scale, parts_ref, target_ref, u_ref, sigma_ref, out_ref):
    n_x, tok, _ = parts_ref.shape
    kvw, rank = u_ref.shape
    out = parts_ref[0]
    for i in range(1, n_x):
        out = out + parts_ref[i]
    sigma = sigma_ref[...]
    u_quant = u_ref[...]
    scaled = (out[:, kvw:] * sigma).astype(jnp.bfloat16)
    residual = out[:, :kvw] + dot32(scaled, u_quant, ((1,), (1,))) - target_ref[...].astype(jnp.float32)
    out_grad = (residual * scale).astype(jnp.bfloat16)
    rank_grad = (dot32(out_grad, u_quant) * sigma).astype(jnp.bfloat16).astype(jnp.float32)
    each = kvw // n_x
    for i in range(n_x):
        out_ref[i, :tok] = rank_grad
        out_ref[i, tok:] = dot32(out_grad[:, i * each : (i + 1) * each], scaled, ((0,), (0,)))


def grads_kernel(tokens_ref, arrived_ref, out_ref):
    n_x, _, rank = arrived_ref.shape
    n_to, packed, _ = out_ref.shape
    tok = tokens_ref.shape[0] // n_x
    v_rows = tokens_ref.shape[1] // n_to
    u_rows = packed - v_rows
    rank_all = jnp.concatenate([arrived_ref[i, :tok] for i in range(n_x)], axis=0)
    rank_all = rank_all.astype(jnp.bfloat16)
    u_sum = arrived_ref[0, tok:]
    for i in range(1, n_x):
        u_sum = u_sum + arrived_ref[i, tok:]
    u_sum = u_sum.astype(jnp.bfloat16)
    repeat = n_to * u_rows // u_sum.shape[0]
    wide = repeat * v_rows
    for j in range(n_to // repeat):
        v_part = dot32(tokens_ref[:, j * wide : (j + 1) * wide], rank_all, ((0,), (0,)))
        v_part = v_part.astype(jnp.bfloat16)
        for i in range(repeat):
            out_ref[j * repeat + i, :v_rows] = v_part[i * v_rows : (i + 1) * v_rows]
            out_ref[j * repeat + i, v_rows:] = u_sum[j * u_rows : (j + 1) * u_rows]


def close_sum_kernel(arrived_ref, out_ref):
    total = arrived_ref[0].astype(jnp.float32)
    for i in range(1, arrived_ref.shape[0]):
        total = total + arrived_ref[i].astype(jnp.float32)
    for i in range(out_ref.shape[0]):
        out_ref[i] = total.astype(out_ref.dtype)


def far_sum_kernel(arrived_ref, v_ref, u_ref):
    n_yh = 2
    v_rows = v_ref.shape[0] // n_yh
    u_rows = u_ref.shape[1] // n_yh
    for h in range(n_yh):
        total = arrived_ref[h].astype(jnp.float32)
        for i in range(h + n_yh, arrived_ref.shape[0], n_yh):
            total = total + arrived_ref[i].astype(jnp.float32)
        v_ref[h * v_rows : (h + 1) * v_rows] = total[:v_rows]
        for i in range(u_ref.shape[0]):
            u_ref[i, h * u_rows : (h + 1) * u_rows] = total[v_rows:]


def place_kernel(order_ref, *refs):
    *piece_refs, out_ref = refs
    n_yh = 2
    rows = piece_refs[0].shape[0] // n_yh
    half = out_ref.shape[0] // n_yh
    for k, piece in enumerate(piece_refs):
        for h in range(n_yh):
            start = pl.multiple_of(h * half + order_ref[k] * rows, rows)
            out_ref[pl.ds(start, rows)] = piece[h * rows : (h + 1) * rows]


def kernel_call(kernel, out, name, operands, scalars=0):
    return pl.pallas_call(
        kernel,
        out_shape=out,
        in_specs=[IN_SMEM] * scalars + [IN_VMEM] * (len(operands) - scalars),
        out_specs=jax.tree.map(lambda _: IN_VMEM, out),
        compiler_params=PARAMS,
        name=name,
    )(*operands)


def shards(hidden, target, base_weight, v_factor, u_factor, sigma, bits, v_exps, u_exps):
    n_x, n_z0, n_near = lax.axis_size("x"), lax.axis_size("z0"), lax.axis_size(NEAR)
    tok, _ = hidden.shape
    kvw, rank = u_factor.shape
    rows = v_factor.shape[0]
    me = lax.axis_index(NEAR)
    swap = [(0, 1), (1, 0)]

    v_quant = fake_quantize(v_factor, bits, v_exps).astype(jnp.bfloat16)
    own = jnp.concatenate([base_weight, v_quant], axis=1)
    across = lax.ppermute(own, "yl", swap)
    pieces = [own, lax.ppermute(own, "core", swap), across, lax.ppermute(across, "core", swap)]
    wide = n_near * rows
    columns = jnp.stack([hidden[:, i * wide : (i + 1) * wide] for i in range(n_x)])
    tokens = exchange(columns, "x").reshape(n_x * tok, wide)
    u_quant = fake_quantize(u_factor, bits, u_exps).astype(jnp.bfloat16)

    f32, bf16 = jnp.float32, jnp.bfloat16
    shape = jax.ShapeDtypeStruct
    order = jnp.bitwise_xor(me, jnp.arange(n_near, dtype=jnp.int32))
    part = kernel_call(
        partial_kernel,
        shape((n_x, tok, kvw + rank), f32),
        "partial_products",
        (order, tokens, *pieces),
        scalars=1,
    )
    scale = 1.0 / math.sqrt(tok * math.prod(lax.axis_size(a) for a in AXES))
    ranks = kernel_call(
        functools.partial(middle_kernel, scale),
        shape((n_x, tok + kvw // n_x, rank), f32),
        "residual_and_grad_u",
        (exchange(part, "x"), target, u_quant, sigma.reshape(1, rank)),
    )
    n_close, n_far = lax.axis_size(CLOSE), lax.axis_size(FAR)
    v_rows, u_rows = wide // n_close, kvw * n_z0 // (n_x * n_close)
    parts = kernel_call(
        grads_kernel,
        shape((n_close, v_rows + u_rows, rank), bf16),
        "grads_packed",
        (tokens, exchange(ranks, "x")),
    )
    mine = kernel_call(
        close_sum_kernel,
        shape((n_far, v_rows + u_rows, rank), bf16),
        "close_sum",
        (exchange(parts, CLOSE),),
    )
    v_mine, u_mine = kernel_call(
        far_sum_kernel,
        (shape((2 * v_rows, rank), f32), shape((lax.axis_size(FSDP), 2 * u_rows, rank), f32)),
        "far_sum",
        (exchange(mine, FAR),),
    )
    grad_u = exchange(u_mine, FSDP).reshape(kvw, rank)
    v_pieces = [v_mine]
    for k in range(1, n_z0):
        v_pieces.append(lax.ppermute(v_mine, "z0", [(j, (j + k) % n_z0) for j in range(n_z0)]))
    order = jnp.remainder(lax.axis_index("z0") - jnp.arange(n_z0, dtype=jnp.int32), n_z0)
    grad_v = kernel_call(
        place_kernel, shape((rows, rank), f32), "grad_v", (order, *v_pieces), scalars=1
    )
    return (grad_v, grad_u)


def solution(mesh):
    fine = Mesh(mesh.devices.reshape(tuple(AXES.values())), tuple(AXES))
    in_specs = (
        P((*DP, *FSDP), None),
        P((*DP, *FSDP), None),
        P(FSDP, None),
        P(FSDP, None),
        P(),
        P(),
        P(),
        P(),
        P(),
    )
    out_specs = (P(FSDP, None), P())
    return jax.shard_map(shards, mesh=fine, in_specs=in_specs, out_specs=out_specs, check_vma=False)
```

```python
import functools
import math

import jax
import jax.numpy as jnp
from jax import lax
from jax.experimental import pallas as pl
from jax.experimental.pallas import tpu as pltpu
from jax.sharding import Mesh, PartitionSpec as P

AXES = {"z1": 4, "z0": 4, "yh": 2, "x": 4, "yl": 2, "core": 2}
DP, FSDP, NEAR = ("z1", "z0", "yh"), ("x", "yl", "core"), ("yl", "core")
CLOSE, FAR = (*NEAR, "yh", "z0"), ("z1", "yh")


def fake_quantize(factor, bits, scale_exps):
    step = jnp.exp2(-scale_exps.astype(jnp.float32))
    upper = jnp.exp2(bits.astype(jnp.float32) - 1.0)
    ratio = factor / step
    smooth = ratio - jnp.sin(2.0 * math.pi * ratio) / (2.0 * math.pi)
    return step * jnp.clip(smooth, -upper, upper - 1.0)


def flips(n, step):
    return [(j, j ^ step) for j in range(n)]


def exchange(parts, axes):
    return lax.all_to_all(parts, axes, 0, 0, tiled=True)


IN_VMEM = pl.BlockSpec(memory_space=pltpu.VMEM)
IN_SMEM = pl.BlockSpec(memory_space=pltpu.SMEM)
PARAMS = pltpu.CompilerParams(vmem_limit_bytes=40 * 1024 * 1024)


def dot32(a, b, dims=((1,), (0,))):
    return lax.dot_general(a, b, (dims, ((), ())), preferred_element_type=jnp.float32)


def partial_kernel(order_ref, tokens_ref, *refs):
    *piece_refs, out_ref = refs
    n_x, tok, _ = out_ref.shape
    rows = piece_refs[0].shape[0]
    for i in range(n_x):
        total = None
        for k, piece in enumerate(piece_refs):
            start = pl.multiple_of(order_ref[k] * rows, rows)
            term = dot32(tokens_ref[i * tok : (i + 1) * tok, pl.ds(start, rows)], piece[...])
            total = term if total is None else total + term
        out_ref[i] = total


def middle_kernel(scale, parts_ref, target_ref, u_ref, sigma_ref, out_ref):
    n_x, tok, _ = parts_ref.shape
    kvw, rank = u_ref.shape
    out = parts_ref[0]
    for i in range(1, n_x):
        out = out + parts_ref[i]
    sigma = sigma_ref[...]
    u_quant = u_ref[...]
    scaled = (out[:, kvw:] * sigma).astype(jnp.bfloat16)
    residual = out[:, :kvw] + dot32(scaled, u_quant, ((1,), (1,))) - target_ref[...].astype(jnp.float32)
    out_grad = (residual * scale).astype(jnp.bfloat16)
    rank_grad = (dot32(out_grad, u_quant) * sigma).astype(jnp.bfloat16).astype(jnp.float32)
    each = kvw // n_x
    for i in range(n_x):
        out_ref[i, :tok] = rank_grad
        out_ref[i, tok:] = dot32(out_grad[:, i * each : (i + 1) * each], scaled, ((0,), (0,)))


def grads_kernel(tokens_ref, arrived_ref, out_ref):
    n_x, _, rank = arrived_ref.shape
    n_to, packed, _ = out_ref.shape
    tok = tokens_ref.shape[0] // n_x
    v_rows = tokens_ref.shape[1] // n_to
    u_rows = packed - v_rows
    rank_all = jnp.concatenate([arrived_ref[i, :tok] for i in range(n_x)], axis=0)
    rank_all = rank_all.astype(jnp.bfloat16)
    u_sum = arrived_ref[0, tok:]
    for i in range(1, n_x):
        u_sum = u_sum + arrived_ref[i, tok:]
    u_sum = u_sum.astype(jnp.bfloat16)
    repeat = n_to * u_rows // u_sum.shape[0]
    wide = repeat * v_rows
    for j in range(n_to // repeat):
        v_part = dot32(tokens_ref[:, j * wide : (j + 1) * wide], rank_all, ((0,), (0,)))
        v_part = v_part.astype(jnp.bfloat16)
        for i in range(repeat):
            out_ref[j * repeat + i, :v_rows] = v_part[i * v_rows : (i + 1) * v_rows]
            out_ref[j * repeat + i, v_rows:] = u_sum[j * u_rows : (j + 1) * u_rows]


def close_sum_kernel(arrived_ref, out_ref):
    total = arrived_ref[0].astype(jnp.float32)
    for i in range(1, arrived_ref.shape[0]):
        total = total + arrived_ref[i].astype(jnp.float32)
    for i in range(out_ref.shape[0]):
        out_ref[i] = total.astype(out_ref.dtype)


def far_sum_kernel(arrived_ref, v_ref, u_ref):
    n_yh = 2
    v_rows = v_ref.shape[0] // n_yh
    u_rows = u_ref.shape[1] // n_yh
    for h in range(n_yh):
        total = arrived_ref[h].astype(jnp.float32)
        for i in range(h + n_yh, arrived_ref.shape[0], n_yh):
            total = total + arrived_ref[i].astype(jnp.float32)
        v_ref[h * v_rows : (h + 1) * v_rows] = total[:v_rows]
        for i in range(u_ref.shape[0]):
            u_ref[i, h * u_rows : (h + 1) * u_rows] = total[v_rows:]


def place_kernel(order_ref, *refs):
    *piece_refs, out_ref = refs
    n_yh, n_z0 = 2, order_ref.shape[0]
    half = out_ref.shape[0] // n_yh
    rows = half // n_z0
    pieces = [p[i : i + rows] for p in piece_refs for i in range(0, p.shape[0], rows)]
    for i, piece in enumerate(pieces):
        start = pl.multiple_of(i % n_yh * half + order_ref[i // n_yh] * rows, rows)
        out_ref[pl.ds(start, rows)] = piece


def kernel_call(kernel, out, name, operands, scalars=0):
    return pl.pallas_call(
        kernel,
        out_shape=out,
        in_specs=[IN_SMEM] * scalars + [IN_VMEM] * (len(operands) - scalars),
        out_specs=jax.tree.map(lambda _: IN_VMEM, out),
        compiler_params=PARAMS,
        name=name,
    )(*operands)


def shards(hidden, target, base_weight, v_factor, u_factor, sigma, bits, v_exps, u_exps):
    n_x, n_z0, n_near = lax.axis_size("x"), lax.axis_size("z0"), lax.axis_size(NEAR)
    tok, _ = hidden.shape
    kvw, rank = u_factor.shape
    rows = v_factor.shape[0]
    me = lax.axis_index(NEAR)
    swap = [(0, 1), (1, 0)]

    v_quant = fake_quantize(v_factor, bits, v_exps).astype(jnp.bfloat16)
    own = jnp.concatenate([base_weight, v_quant], axis=1)
    across = lax.ppermute(own, "yl", swap)
    pieces = [own, lax.ppermute(own, "core", swap), across, lax.ppermute(across, "core", swap)]
    wide = n_near * rows
    columns = jnp.stack([hidden[:, i * wide : (i + 1) * wide] for i in range(n_x)])
    tokens = exchange(columns, "x").reshape(n_x * tok, wide)
    u_quant = fake_quantize(u_factor, bits, u_exps).astype(jnp.bfloat16)

    f32, bf16 = jnp.float32, jnp.bfloat16
    shape = jax.ShapeDtypeStruct
    order = jnp.bitwise_xor(me, jnp.arange(n_near, dtype=jnp.int32))
    part = kernel_call(
        partial_kernel,
        shape((n_x, tok, kvw + rank), f32),
        "partial_products",
        (order, tokens, *pieces),
        scalars=1,
    )
    scale = 1.0 / math.sqrt(tok * math.prod(lax.axis_size(a) for a in AXES))
    ranks = kernel_call(
        functools.partial(middle_kernel, scale),
        shape((n_x, tok + kvw // n_x, rank), f32),
        "residual_and_grad_u",
        (exchange(part, "x"), target, u_quant, sigma.reshape(1, rank)),
    )
    n_close, n_far = lax.axis_size(CLOSE), lax.axis_size(FAR)
    v_rows, u_rows = wide // n_close, kvw * n_z0 // (n_x * n_close)
    parts = kernel_call(
        grads_kernel,
        shape((n_close, v_rows + u_rows, rank), bf16),
        "grads_packed",
        (tokens, exchange(ranks, "x")),
    )
    mine = kernel_call(
        close_sum_kernel,
        shape((n_far, v_rows + u_rows, rank), bf16),
        "close_sum",
        (exchange(parts, CLOSE),),
    )
    v_mine, u_mine = kernel_call(
        far_sum_kernel,
        (shape((2 * v_rows, rank), f32), shape((lax.axis_size(FSDP), 2 * u_rows, rank), f32)),
        "far_sum",
        (exchange(mine, FAR),),
    )
    grad_u = exchange(u_mine, FSDP).reshape(kvw, rank)
    v_two = jnp.concatenate([v_mine, lax.ppermute(v_mine, "z0", flips(n_z0, 2))], axis=0)
    v_pieces = [v_two, lax.ppermute(v_two, "z0", flips(n_z0, 1))]
    order = jnp.bitwise_xor(lax.axis_index("z0"), jnp.array([0, 2, 1, 3], jnp.int32))
    grad_v = kernel_call(
        place_kernel, shape((rows, rank), f32), "grad_v", (order, *v_pieces), scalars=1
    )
    return (grad_v, grad_u)


def solution(mesh):
    fine = Mesh(mesh.devices.reshape(tuple(AXES.values())), tuple(AXES))
    in_specs = (
        P((*DP, *FSDP), None),
        P((*DP, *FSDP), None),
        P(FSDP, None),
        P(FSDP, None),
        P(),
        P(),
        P(),
        P(),
        P(),
    )
    out_specs = (P(FSDP, None), P())
    return jax.shard_map(shards, mesh=fine, in_specs=in_specs, out_specs=out_specs, check_vma=False)
```

```python
import functools
import math

import jax
import jax.numpy as jnp
from jax import lax
from jax.experimental import pallas as pl
from jax.experimental.pallas import tpu as pltpu
from jax.sharding import Mesh, PartitionSpec as P

AXES = {"z1": 4, "z0": 4, "yh": 2, "x": 4, "yl": 2, "core": 2}
DP, FSDP, NEAR = ("z1", "z0", "yh"), ("x", "yl", "core"), ("yl", "core")
CLOSE, FAR = ("yl", "yh", "z0"), ("z1", "yh")
SPLIT = ("x", "core", "yl")


def fake_quantize(factor, bits, scale_exps):
    step = jnp.exp2(-scale_exps.astype(jnp.float32))
    upper = jnp.exp2(bits.astype(jnp.float32) - 1.0)
    ratio = factor / step
    smooth = ratio - jnp.sin(2.0 * math.pi * ratio) / (2.0 * math.pi)
    return step * jnp.clip(smooth, -upper, upper - 1.0)


def flips(n, step):
    return [(j, j ^ step) for j in range(n)]


def exchange(parts, axes):
    return lax.all_to_all(parts, axes, 0, 0, tiled=True)


IN_VMEM = pl.BlockSpec(memory_space=pltpu.VMEM)
IN_SMEM = pl.BlockSpec(memory_space=pltpu.SMEM)
PARAMS = pltpu.CompilerParams(vmem_limit_bytes=40 * 1024 * 1024)


def dot32(a, b, dims=((1,), (0,))):
    return lax.dot_general(a, b, (dims, ((), ())), preferred_element_type=jnp.float32)


def partial_kernel(order_ref, tokens_ref, *refs):
    *piece_refs, out_ref = refs
    n_x, tok, _ = out_ref.shape
    rows = piece_refs[0].shape[0]
    for i in range(n_x):
        total = None
        for k, piece in enumerate(piece_refs):
            start = pl.multiple_of(order_ref[k] * rows, rows)
            term = dot32(tokens_ref[i * tok : (i + 1) * tok, pl.ds(start, rows)], piece[...])
            total = term if total is None else total + term
        out_ref[i] = total


def middle_kernel(scale, parts_ref, target_ref, u_ref, sigma_ref, out_ref):
    n_x, tok, _ = parts_ref.shape
    kvw, rank = u_ref.shape
    out = parts_ref[0]
    for i in range(1, n_x):
        out = out + parts_ref[i]
    sigma = sigma_ref[...]
    u_quant = u_ref[...]
    scaled = (out[:, kvw:] * sigma).astype(jnp.bfloat16)
    residual = out[:, :kvw] + dot32(scaled, u_quant, ((1,), (1,))) - target_ref[...].astype(jnp.float32)
    out_grad = (residual * scale).astype(jnp.bfloat16)
    rank_grad = (dot32(out_grad, u_quant) * sigma).astype(jnp.bfloat16)
    grad_u = dot32(out_grad, scaled, ((0,), (0,)))
    high = grad_u.astype(jnp.bfloat16)
    low = (grad_u - high.astype(jnp.float32)).astype(jnp.bfloat16)
    n_to = out_ref.shape[0]
    each = kvw // n_to
    for i in range(n_to):
        out_ref[i, :tok] = rank_grad
        out_ref[i, tok : tok + each] = high[i * each : (i + 1) * each]
        out_ref[i, tok + each :] = low[i * each : (i + 1) * each]


def grads_kernel(core_ref, tokens_ref, others_ref, arrived_ref, out_ref):
    core = core_ref[0]
    n_from, both, rank = arrived_ref.shape
    n_to, packed, _ = out_ref.shape
    n_x, n_yl = n_from // 2, 2
    rows = others_ref.shape[1] // n_yl
    tok = tokens_ref.shape[0] // n_x
    each = (both - tok) // 2
    per_yl = n_to // n_yl
    v_rows = rows // per_yl
    u_rows = packed - v_rows
    mine = jnp.concatenate([arrived_ref[2 * x + core, :tok] for x in range(n_x)], axis=0)
    other = jnp.concatenate([arrived_ref[2 * x + 1 - core, :tok] for x in range(n_x)], axis=0)
    u_sum = jnp.zeros((each, rank), jnp.float32)
    for i in range(n_from):
        u_sum = u_sum + arrived_ref[i, tok : tok + each].astype(jnp.float32)
        u_sum = u_sum + arrived_ref[i, tok + each :].astype(jnp.float32)
    u_sum = u_sum.astype(jnp.bfloat16)
    repeat = n_to * u_rows // each
    for j in range(n_yl):
        start = pl.multiple_of((2 * j + core) * rows, rows)
        v_part = dot32(tokens_ref[:, pl.ds(start, rows)], mine, ((0,), (0,)))
        v_part = v_part + dot32(others_ref[:, j * rows : (j + 1) * rows], other, ((0,), (0,)))
        v_part = v_part.astype(jnp.bfloat16)
        for r in range(per_yl):
            i = j * per_yl + r
            u_at = i // repeat * u_rows
            out_ref[i, :v_rows] = v_part[r * v_rows : (r + 1) * v_rows]
            out_ref[i, v_rows:] = u_sum[u_at : u_at + u_rows]


def close_sum_kernel(arrived_ref, out_ref):
    total = arrived_ref[0].astype(jnp.float32)
    for i in range(1, arrived_ref.shape[0]):
        total = total + arrived_ref[i].astype(jnp.float32)
    for i in range(out_ref.shape[0]):
        out_ref[i] = total.astype(out_ref.dtype)


def far_sum_kernel(arrived_ref, v_ref, u_ref):
    n_yh = 2
    v_rows = v_ref.shape[0] // n_yh
    u_rows = u_ref.shape[1] // n_yh
    for h in range(n_yh):
        total = arrived_ref[h].astype(jnp.float32)
        for i in range(h + n_yh, arrived_ref.shape[0], n_yh):
            total = total + arrived_ref[i].astype(jnp.float32)
        v_ref[h * v_rows : (h + 1) * v_rows] = total[:v_rows]
        for i in range(u_ref.shape[0]):
            u_ref[i, h * u_rows : (h + 1) * u_rows] = total[v_rows:]


def place_kernel(order_ref, *refs):
    *piece_refs, out_ref = refs
    n_yh, n_z0 = 2, order_ref.shape[0]
    half = out_ref.shape[0] // n_yh
    rows = half // n_z0
    pieces = [p[i : i + rows] for p in piece_refs for i in range(0, p.shape[0], rows)]
    for i, piece in enumerate(pieces):
        start = pl.multiple_of(i % n_yh * half + order_ref[i // n_yh] * rows, rows)
        out_ref[pl.ds(start, rows)] = piece


def kernel_call(kernel, out, name, operands, scalars=0):
    return pl.pallas_call(
        kernel,
        out_shape=out,
        in_specs=[IN_SMEM] * scalars + [IN_VMEM] * (len(operands) - scalars),
        out_specs=jax.tree.map(lambda _: IN_VMEM, out),
        compiler_params=PARAMS,
        name=name,
    )(*operands)


def shards(hidden, target, base_weight, v_factor, u_factor, sigma, bits, v_exps, u_exps):
    n_x, n_z0, n_near = lax.axis_size("x"), lax.axis_size("z0"), lax.axis_size(NEAR)
    tok, _ = hidden.shape
    kvw, rank = u_factor.shape
    rows = v_factor.shape[0]
    me = lax.axis_index(NEAR)
    swap = [(0, 1), (1, 0)]

    v_quant = fake_quantize(v_factor, bits, v_exps).astype(jnp.bfloat16)
    own = jnp.concatenate([base_weight, v_quant], axis=1)
    across = lax.ppermute(own, "yl", swap)
    pieces = [own, lax.ppermute(own, "core", swap), across, lax.ppermute(across, "core", swap)]
    wide = n_near * rows
    columns = jnp.stack([hidden[:, i * wide : (i + 1) * wide] for i in range(n_x)])
    tokens = exchange(columns, "x").reshape(n_x * tok, wide)
    u_quant = fake_quantize(u_factor, bits, u_exps).astype(jnp.bfloat16)

    f32, bf16 = jnp.float32, jnp.bfloat16
    shape = jax.ShapeDtypeStruct
    order = jnp.bitwise_xor(me, jnp.arange(n_near, dtype=jnp.int32))
    part = kernel_call(
        partial_kernel,
        shape((n_x, tok, kvw + rank), f32),
        "partial_products",
        (order, tokens, *pieces),
        scalars=1,
    )
    core = lax.axis_index("core")
    others = [
        lax.dynamic_slice_in_dim(tokens, (2 * i + 1 - core) * rows, rows, 1)
        for i in range(n_near // 2)
    ]
    others = lax.ppermute(jnp.concatenate(others, axis=1), "core", swap)
    scale = 1.0 / math.sqrt(tok * math.prod(lax.axis_size(a) for a in AXES))
    ranks = kernel_call(
        functools.partial(middle_kernel, scale),
        shape((2 * n_x, tok + kvw // n_x, rank), bf16),
        "residual_and_grad_u",
        (exchange(part, "x"), target, u_quant, sigma.reshape(1, rank)),
    )
    n_close, n_far = lax.axis_size(CLOSE), lax.axis_size(FAR)
    v_rows, u_rows = wide // (2 * n_close), kvw * n_z0 // (2 * n_x * n_close)
    parts = kernel_call(
        grads_kernel,
        shape((n_close, v_rows + u_rows, rank), bf16),
        "grads_packed",
        (core.reshape(1), tokens, others, exchange(ranks, ("x", "core"))),
        scalars=1,
    )
    mine = kernel_call(
        close_sum_kernel,
        shape((n_far, v_rows + u_rows, rank), bf16),
        "close_sum",
        (exchange(parts, CLOSE),),
    )
    v_mine, u_mine = kernel_call(
        far_sum_kernel,
        (shape((2 * v_rows, rank), f32), shape((lax.axis_size(SPLIT), 2 * u_rows, rank), f32)),
        "far_sum",
        (exchange(mine, FAR),),
    )
    grad_u = exchange(u_mine, SPLIT).reshape(kvw, rank)
    v_two = jnp.concatenate([v_mine, lax.ppermute(v_mine, "z0", flips(n_z0, 2))], axis=0)
    v_pieces = [v_two, lax.ppermute(v_two, "z0", flips(n_z0, 1))]
    order = jnp.bitwise_xor(lax.axis_index("z0"), jnp.array([0, 2, 1, 3], jnp.int32))
    grad_v = kernel_call(
        place_kernel, shape((rows, rank), f32), "grad_v", (order, *v_pieces), scalars=1
    )
    return (grad_v, grad_u)


def solution(mesh):
    fine = Mesh(mesh.devices.reshape(tuple(AXES.values())), tuple(AXES))
    in_specs = (
        P((*DP, *FSDP), None),
        P((*DP, *FSDP), None),
        P(FSDP, None),
        P(FSDP, None),
        P(),
        P(),
        P(),
        P(),
        P(),
    )
    out_specs = (P(FSDP, None), P())
    return jax.shard_map(shards, mesh=fine, in_specs=in_specs, out_specs=out_specs, check_vma=False)
```

```python
import functools
import math

import jax
import jax.numpy as jnp
from jax import lax
from jax.experimental import pallas as pl
from jax.experimental.pallas import tpu as pltpu
from jax.sharding import Mesh, PartitionSpec as P

AXES = {"z1": 4, "z0": 4, "yh": 2, "x": 4, "yl": 2, "core": 2}
DP, FSDP, NEAR = ("z1", "z0", "yh"), ("x", "yl", "core"), ("yl", "core")
CLOSE, FAR = ("yl", "yh", "z0"), ("z1", "yh")
SPLIT = ("x", "core", "yl")


def fake_quantize(factor, bits, scale_exps):
    step = jnp.exp2(-scale_exps.astype(jnp.float32))
    upper = jnp.exp2(bits.astype(jnp.float32) - 1.0)
    ratio = factor / step
    smooth = ratio - jnp.sin(2.0 * math.pi * ratio) / (2.0 * math.pi)
    return step * jnp.clip(smooth, -upper, upper - 1.0)


def flips(n, step):
    return [(j, j ^ step) for j in range(n)]


def exchange(parts, axes):
    return lax.all_to_all(parts, axes, 0, 0, tiled=True)


IN_VMEM = pl.BlockSpec(memory_space=pltpu.VMEM)
IN_SMEM = pl.BlockSpec(memory_space=pltpu.SMEM)
PARAMS = pltpu.CompilerParams(vmem_limit_bytes=40 * 1024 * 1024)


def dot32(a, b, dims=((1,), (0,))):
    return lax.dot_general(a, b, (dims, ((), ())), preferred_element_type=jnp.float32)


def partial_kernel(order_ref, tokens_ref, *refs):
    *piece_refs, out_ref = refs
    n_x, tok, _ = out_ref.shape
    rows = piece_refs[0].shape[0]
    for i in range(n_x):
        total = None
        for k, piece in enumerate(piece_refs):
            start = pl.multiple_of(order_ref[k] * rows, rows)
            term = dot32(tokens_ref[i * tok : (i + 1) * tok, pl.ds(start, rows)], piece[...])
            total = term if total is None else total + term
        out_ref[i] = total


def middle_kernel(scale, parts_ref, target_ref, u_ref, sigma_ref, out_ref):
    n_x, tok, _ = parts_ref.shape
    kvw, rank = u_ref.shape
    out = parts_ref[0]
    for i in range(1, n_x):
        out = out + parts_ref[i]
    sigma = sigma_ref[...]
    u_quant = u_ref[...]
    scaled = (out[:, kvw:] * sigma).astype(jnp.bfloat16)
    residual = out[:, :kvw] + dot32(scaled, u_quant, ((1,), (1,))) - target_ref[...].astype(jnp.float32)
    out_grad = (residual * scale).astype(jnp.bfloat16)
    rank_grad = (dot32(out_grad, u_quant) * sigma).astype(jnp.bfloat16)
    grad_u = dot32(out_grad, scaled, ((0,), (0,)))
    high = grad_u.astype(jnp.bfloat16)
    low = (grad_u - high.astype(jnp.float32)).astype(jnp.bfloat16)
    n_to = out_ref.shape[0]
    each = kvw // n_to
    for i in range(n_to):
        out_ref[i, :tok] = rank_grad
        out_ref[i, tok : tok + each] = high[i * each : (i + 1) * each]
        out_ref[i, tok + each :] = low[i * each : (i + 1) * each]


def grads_kernel(core_ref, tokens_ref, others_ref, arrived_ref, out_ref):
    core = core_ref[0]
    n_from, both, rank = arrived_ref.shape
    n_to, packed, _ = out_ref.shape
    n_x, n_yl = n_from // 2, 2
    rows = others_ref.shape[1] // n_yl
    tok = tokens_ref.shape[0] // n_x
    each = (both - tok) // 2
    per_yl = n_to // n_yl
    v_rows = rows // per_yl
    u_rows = packed - v_rows
    mine = jnp.concatenate([arrived_ref[2 * x + core, :tok] for x in range(n_x)], axis=0)
    other = jnp.concatenate([arrived_ref[2 * x + 1 - core, :tok] for x in range(n_x)], axis=0)
    u_sum = jnp.zeros((each, rank), jnp.float32)
    for i in range(n_from):
        u_sum = u_sum + arrived_ref[i, tok : tok + each].astype(jnp.float32)
        u_sum = u_sum + arrived_ref[i, tok + each :].astype(jnp.float32)
    u_sum = u_sum.astype(jnp.bfloat16)
    repeat = n_to * u_rows // each
    for j in range(n_yl):
        start = pl.multiple_of((2 * j + core) * rows, rows)
        v_part = dot32(tokens_ref[:, pl.ds(start, rows)], mine, ((0,), (0,)))
        v_part = v_part + dot32(others_ref[:, j * rows : (j + 1) * rows], other, ((0,), (0,)))
        v_part = v_part.astype(jnp.bfloat16)
        for r in range(per_yl):
            i = j * per_yl + r
            u_at = i // repeat * u_rows
            out_ref[i, :v_rows] = v_part[r * v_rows : (r + 1) * v_rows]
            out_ref[i, v_rows:] = u_sum[u_at : u_at + u_rows]


def close_sum_kernel(arrived_ref, out_ref):
    total = arrived_ref[0].astype(jnp.float32)
    for i in range(1, arrived_ref.shape[0]):
        total = total + arrived_ref[i].astype(jnp.float32)
    for i in range(out_ref.shape[0]):
        out_ref[i] = total.astype(out_ref.dtype)


def far_v_kernel(arrived_ref, v_ref):
    n_yh = 2
    rows = v_ref.shape[0] // n_yh
    for h in range(n_yh):
        total = arrived_ref[h, :rows].astype(jnp.float32)
        for i in range(h + n_yh, arrived_ref.shape[0], n_yh):
            total = total + arrived_ref[i, :rows].astype(jnp.float32)
        v_ref[h * rows : (h + 1) * rows] = total


def far_u_kernel(arrived_ref, v_ref, u_ref):
    n_yh = 2
    v_rows = v_ref.shape[0] // n_yh
    rows = u_ref.shape[1] // n_yh
    for h in range(n_yh):
        total = arrived_ref[h, v_rows:].astype(jnp.float32)
        for i in range(h + n_yh, arrived_ref.shape[0], n_yh):
            total = total + arrived_ref[i, v_rows:].astype(jnp.float32)
        for i in range(u_ref.shape[0]):
            u_ref[i, h * rows : (h + 1) * rows] = total


def place_kernel(order_ref, *refs):
    *piece_refs, out_ref = refs
    n_yh, n_z0 = 2, order_ref.shape[0]
    half = out_ref.shape[0] // n_yh
    rows = half // n_z0
    pieces = [p[i : i + rows] for p in piece_refs for i in range(0, p.shape[0], rows)]
    for i, piece in enumerate(pieces):
        start = pl.multiple_of(i % n_yh * half + order_ref[i // n_yh] * rows, rows)
        out_ref[pl.ds(start, rows)] = piece


def kernel_call(kernel, out, name, operands, scalars=0):
    return pl.pallas_call(
        kernel,
        out_shape=out,
        in_specs=[IN_SMEM] * scalars + [IN_VMEM] * (len(operands) - scalars),
        out_specs=jax.tree.map(lambda _: IN_VMEM, out),
        compiler_params=PARAMS,
        name=name,
    )(*operands)


def shards(hidden, target, base_weight, v_factor, u_factor, sigma, bits, v_exps, u_exps):
    n_x, n_z0, n_near = lax.axis_size("x"), lax.axis_size("z0"), lax.axis_size(NEAR)
    tok, _ = hidden.shape
    kvw, rank = u_factor.shape
    rows = v_factor.shape[0]
    me = lax.axis_index(NEAR)
    swap = [(0, 1), (1, 0)]

    v_quant = fake_quantize(v_factor, bits, v_exps).astype(jnp.bfloat16)
    own = jnp.concatenate([base_weight, v_quant], axis=1)
    across = lax.ppermute(own, "yl", swap)
    pieces = [own, lax.ppermute(own, "core", swap), across, lax.ppermute(across, "core", swap)]
    wide = n_near * rows
    columns = jnp.stack([hidden[:, i * wide : (i + 1) * wide] for i in range(n_x)])
    tokens = exchange(columns, "x").reshape(n_x * tok, wide)
    u_quant = fake_quantize(u_factor, bits, u_exps).astype(jnp.bfloat16)

    f32, bf16 = jnp.float32, jnp.bfloat16
    shape = jax.ShapeDtypeStruct
    order = jnp.bitwise_xor(me, jnp.arange(n_near, dtype=jnp.int32))
    part = kernel_call(
        partial_kernel,
        shape((n_x, tok, kvw + rank), f32),
        "partial_products",
        (order, tokens, *pieces),
        scalars=1,
    )
    core = lax.axis_index("core")
    others = [
        lax.dynamic_slice_in_dim(tokens, (2 * i + 1 - core) * rows, rows, 1)
        for i in range(n_near // 2)
    ]
    others = lax.ppermute(jnp.concatenate(others, axis=1), "core", swap)
    out_parts, others = lax.optimization_barrier((exchange(part, "x"), others))
    scale = 1.0 / math.sqrt(tok * math.prod(lax.axis_size(a) for a in AXES))
    ranks = kernel_call(
        functools.partial(middle_kernel, scale),
        shape((2 * n_x, tok + kvw // n_x, rank), bf16),
        "residual_and_grad_u",
        (out_parts, target, u_quant, sigma.reshape(1, rank)),
    )
    n_close, n_far = lax.axis_size(CLOSE), lax.axis_size(FAR)
    v_rows, u_rows = wide // (2 * n_close), kvw * n_z0 // (2 * n_x * n_close)
    parts = kernel_call(
        grads_kernel,
        shape((n_close, v_rows + u_rows, rank), bf16),
        "grads_packed",
        (core.reshape(1), tokens, others, exchange(ranks, ("x", "core"))),
        scalars=1,
    )
    mine = kernel_call(
        close_sum_kernel,
        shape((n_far, v_rows + u_rows, rank), bf16),
        "close_sum",
        (exchange(parts, CLOSE),),
    )
    arrived = exchange(mine, FAR)
    v_mine = kernel_call(far_v_kernel, shape((2 * v_rows, rank), f32), "far_v", (arrived,))
    u_mine = kernel_call(
        far_u_kernel,
        shape((lax.axis_size(SPLIT), 2 * u_rows, rank), f32),
        "far_u",
        (arrived, v_mine),
    )
    grad_u = exchange(u_mine, SPLIT).reshape(kvw, rank)
    v_two = jnp.concatenate([v_mine, lax.ppermute(v_mine, "z0", flips(n_z0, 2))], axis=0)
    v_pieces = [v_two, lax.ppermute(v_two, "z0", flips(n_z0, 1))]
    order = jnp.bitwise_xor(lax.axis_index("z0"), jnp.array([0, 2, 1, 3], jnp.int32))
    grad_v = kernel_call(
        place_kernel, shape((rows, rank), f32), "grad_v", (order, *v_pieces), scalars=1
    )
    return (grad_v, grad_u)


def solution(mesh):
    fine = Mesh(mesh.devices.reshape(tuple(AXES.values())), tuple(AXES))
    in_specs = (
        P((*DP, *FSDP), None),
        P((*DP, *FSDP), None),
        P(FSDP, None),
        P(FSDP, None),
        P(),
        P(),
        P(),
        P(),
        P(),
    )
    out_specs = (P(FSDP, None), P())
    return jax.shard_map(shards, mesh=fine, in_specs=in_specs, out_specs=out_specs, check_vma=False)
```

```python
import functools
import math

import jax
import jax.numpy as jnp
from jax import lax
from jax.experimental import pallas as pl
from jax.experimental.pallas import tpu as pltpu
from jax.sharding import Mesh, PartitionSpec as P

AXES = {"z1": 4, "z0": 4, "yh": 2, "x": 4, "yl": 2, "core": 2}
DP, FSDP, NEAR = ("z1", "z0", "yh"), ("x", "yl", "core"), ("yl", "core")
CLOSE, FAR = ("yl", "yh", "z0"), ("z1", "yh")
SPLIT = ("x", "core", "yl")


def fake_quantize(factor, bits, scale_exps):
    step = jnp.exp2(-scale_exps.astype(jnp.float32))
    upper = jnp.exp2(bits.astype(jnp.float32) - 1.0)
    ratio = factor / step
    smooth = ratio - jnp.sin(2.0 * math.pi * ratio) / (2.0 * math.pi)
    return step * jnp.clip(smooth, -upper, upper - 1.0)


def flips(n, step):
    return [(j, j ^ step) for j in range(n)]


def exchange(parts, axes):
    return lax.all_to_all(parts, axes, 0, 0, tiled=True)


IN_VMEM = pl.BlockSpec(memory_space=pltpu.VMEM)
IN_SMEM = pl.BlockSpec(memory_space=pltpu.SMEM)
PARAMS = pltpu.CompilerParams(vmem_limit_bytes=40 * 1024 * 1024)


def dot32(a, b, dims=((1,), (0,))):
    return lax.dot_general(a, b, (dims, ((), ())), preferred_element_type=jnp.float32)


def partial_kernel(order_ref, tokens_ref, *refs):
    *piece_refs, out_ref = refs
    n_x, tok, _ = out_ref.shape
    rows = piece_refs[0].shape[0]
    for i in range(n_x):
        total = None
        for k, piece in enumerate(piece_refs):
            start = pl.multiple_of(order_ref[k] * rows, rows)
            term = dot32(tokens_ref[i * tok : (i + 1) * tok, pl.ds(start, rows)], piece[...])
            total = term if total is None else total + term
        out_ref[i] = total


def middle_kernel(scale, parts_ref, target_ref, u_ref, sigma_ref, out_ref):
    n_x, tok, _ = parts_ref.shape
    kvw, rank = u_ref.shape
    out = parts_ref[0]
    for i in range(1, n_x):
        out = out + parts_ref[i]
    sigma = sigma_ref[...]
    u_quant = u_ref[...]
    scaled = (out[:, kvw:] * sigma).astype(jnp.bfloat16)
    residual = out[:, :kvw] + dot32(scaled, u_quant, ((1,), (1,))) - target_ref[...].astype(jnp.float32)
    out_grad = (residual * scale).astype(jnp.bfloat16)
    rank_grad = (dot32(out_grad, u_quant) * sigma).astype(jnp.bfloat16)
    grad_u = dot32(out_grad, scaled, ((0,), (0,)))
    high = grad_u.astype(jnp.bfloat16)
    low = (grad_u - high.astype(jnp.float32)).astype(jnp.bfloat16)
    n_to = out_ref.shape[0]
    each = kvw // n_to
    for i in range(n_to):
        out_ref[i, :tok] = rank_grad
        out_ref[i, tok : tok + each] = high[i * each : (i + 1) * each]
        out_ref[i, tok + each :] = low[i * each : (i + 1) * each]


def grads_kernel(core_ref, tokens_ref, others_ref, arrived_ref, out_ref):
    core = core_ref[0]
    n_from, both, rank = arrived_ref.shape
    n_to, packed, _ = out_ref.shape
    n_x, n_yl = n_from // 2, 2
    rows = others_ref.shape[1] // n_yl
    tok = tokens_ref.shape[0] // n_x
    each = (both - tok) // 2
    per_yl = n_to // n_yl
    v_rows = rows // per_yl
    u_rows = packed - v_rows
    mine = jnp.concatenate([arrived_ref[2 * x + core, :tok] for x in range(n_x)], axis=0)
    other = jnp.concatenate([arrived_ref[2 * x + 1 - core, :tok] for x in range(n_x)], axis=0)
    u_sum = jnp.zeros((each, rank), jnp.float32)
    for i in range(n_from):
        u_sum = u_sum + arrived_ref[i, tok : tok + each].astype(jnp.float32)
        u_sum = u_sum + arrived_ref[i, tok + each :].astype(jnp.float32)
    u_sum = u_sum.astype(jnp.bfloat16)
    repeat = n_to * u_rows // each
    for j in range(n_yl):
        start = pl.multiple_of((2 * j + core) * rows, rows)
        v_part = dot32(tokens_ref[:, pl.ds(start, rows)], mine, ((0,), (0,)))
        v_part = v_part + dot32(others_ref[:, j * rows : (j + 1) * rows], other, ((0,), (0,)))
        v_part = v_part.astype(jnp.bfloat16)
        for r in range(per_yl):
            i = j * per_yl + r
            u_at = i // repeat * u_rows
            out_ref[i, :v_rows] = v_part[r * v_rows : (r + 1) * v_rows]
            out_ref[i, v_rows:] = u_sum[u_at : u_at + u_rows]


def close_sum_kernel(arrived_ref, out_ref):
    total = arrived_ref[0].astype(jnp.float32)
    for i in range(1, arrived_ref.shape[0]):
        total = total + arrived_ref[i].astype(jnp.float32)
    for i in range(out_ref.shape[0]):
        out_ref[i] = total.astype(out_ref.dtype)


def far_v_kernel(arrived_ref, v_ref):
    n_yh = 2
    rows = v_ref.shape[0] // n_yh
    for h in range(n_yh):
        total = arrived_ref[h, :rows].astype(jnp.float32)
        for i in range(h + n_yh, arrived_ref.shape[0], n_yh):
            total = total + arrived_ref[i, :rows].astype(jnp.float32)
        v_ref[h * rows : (h + 1) * rows] = total


def far_u_kernel(arrived_ref, v_ref, u_ref):
    n_yh = 2
    v_rows = v_ref.shape[0] // n_yh
    rows = u_ref.shape[1] // n_yh
    for h in range(n_yh):
        total = arrived_ref[h, v_rows:].astype(jnp.float32)
        for i in range(h + n_yh, arrived_ref.shape[0], n_yh):
            total = total + arrived_ref[i, v_rows:].astype(jnp.float32)
        for i in range(u_ref.shape[0]):
            u_ref[i, h * rows : (h + 1) * rows] = total


def place_kernel(order_ref, u_ref, *refs):
    *piece_refs, v_ref, out_u_ref = refs
    n_yh, n_z0 = 2, order_ref.shape[0]
    half = v_ref.shape[0] // n_yh
    rows = half // n_z0
    pieces = [p[i : i + rows] for p in piece_refs for i in range(0, p.shape[0], rows)]
    for i, piece in enumerate(pieces):
        start = pl.multiple_of(i % n_yh * half + order_ref[i // n_yh] * rows, rows)
        v_ref[pl.ds(start, rows)] = piece
    out_u_ref[...] = u_ref[...]


def kernel_call(kernel, out, name, operands, scalars=0):
    return pl.pallas_call(
        kernel,
        out_shape=out,
        in_specs=[IN_SMEM] * scalars + [IN_VMEM] * (len(operands) - scalars),
        out_specs=jax.tree.map(lambda _: IN_VMEM, out),
        compiler_params=PARAMS,
        name=name,
    )(*operands)


def shards(hidden, target, base_weight, v_factor, u_factor, sigma, bits, v_exps, u_exps):
    n_x, n_z0, n_near = lax.axis_size("x"), lax.axis_size("z0"), lax.axis_size(NEAR)
    tok, _ = hidden.shape
    kvw, rank = u_factor.shape
    rows = v_factor.shape[0]
    me = lax.axis_index(NEAR)
    swap = [(0, 1), (1, 0)]

    v_quant = fake_quantize(v_factor, bits, v_exps).astype(jnp.bfloat16)
    own = jnp.concatenate([base_weight, v_quant], axis=1)
    across = lax.ppermute(own, "yl", swap)
    pieces = [own, lax.ppermute(own, "core", swap), across, lax.ppermute(across, "core", swap)]
    wide = n_near * rows
    columns = lax.all_to_all(hidden.reshape(tok, n_x, wide), "x", 1, 1, tiled=True)
    tokens = columns.transpose(1, 0, 2).reshape(n_x * tok, wide)
    u_quant = fake_quantize(u_factor, bits, u_exps).astype(jnp.bfloat16)

    f32, bf16 = jnp.float32, jnp.bfloat16
    shape = jax.ShapeDtypeStruct
    order = jnp.bitwise_xor(me, jnp.arange(n_near, dtype=jnp.int32))
    part = kernel_call(
        partial_kernel,
        shape((n_x, tok, kvw + rank), f32),
        "partial_products",
        (order, tokens, *pieces),
        scalars=1,
    )
    core = lax.axis_index("core")
    others = [
        lax.dynamic_slice_in_dim(tokens, (2 * i + 1 - core) * rows, rows, 1)
        for i in range(n_near // 2)
    ]
    others = lax.ppermute(jnp.concatenate(others, axis=1), "core", swap)
    scale = 1.0 / math.sqrt(tok * math.prod(lax.axis_size(a) for a in AXES))
    ranks = kernel_call(
        functools.partial(middle_kernel, scale),
        shape((2 * n_x, tok + kvw // n_x, rank), bf16),
        "residual_and_grad_u",
        (exchange(part, "x"), target, u_quant, sigma.reshape(1, rank)),
    )
    ranks, others = lax.optimization_barrier((ranks, others))
    n_close, n_far = lax.axis_size(CLOSE), lax.axis_size(FAR)
    v_rows, u_rows = wide // (2 * n_close), kvw * n_z0 // (2 * n_x * n_close)
    parts = kernel_call(
        grads_kernel,
        shape((n_close, v_rows + u_rows, rank), bf16),
        "grads_packed",
        (core.reshape(1), tokens, others, exchange(ranks, ("x", "core"))),
        scalars=1,
    )
    mine = kernel_call(
        close_sum_kernel,
        shape((n_far, v_rows + u_rows, rank), bf16),
        "close_sum",
        (exchange(parts, CLOSE),),
    )
    arrived = exchange(mine, FAR)
    v_mine = kernel_call(far_v_kernel, shape((2 * v_rows, rank), f32), "far_v", (arrived,))
    u_mine = kernel_call(
        far_u_kernel,
        shape((lax.axis_size(SPLIT), 2 * u_rows, rank), f32),
        "far_u",
        (arrived, v_mine),
    )
    grad_u = exchange(u_mine, SPLIT).reshape(kvw, rank)
    v_two = jnp.concatenate([v_mine, lax.ppermute(v_mine, "z0", flips(n_z0, 2))], axis=0)
    v_pieces = [v_two, lax.ppermute(v_two, "z0", flips(n_z0, 1))]
    order = jnp.bitwise_xor(lax.axis_index("z0"), jnp.array([0, 2, 1, 3], jnp.int32))
    return kernel_call(
        place_kernel,
        (shape((rows, rank), f32), shape((kvw, rank), f32)),
        "grads",
        (order, grad_u, *v_pieces),
        scalars=1,
    )


def solution(mesh):
    fine = Mesh(mesh.devices.reshape(tuple(AXES.values())), tuple(AXES))
    in_specs = (
        P((*DP, *FSDP), None),
        P((*DP, *FSDP), None),
        P(FSDP, None),
        P(FSDP, None),
        P(),
        P(),
        P(),
        P(),
        P(),
    )
    out_specs = (P(FSDP, None), P())
    return jax.shard_map(shards, mesh=fine, in_specs=in_specs, out_specs=out_specs, check_vma=False)
```

```python
import functools
import math

import jax
import jax.numpy as jnp
from jax import lax
from jax.experimental import pallas as pl
from jax.experimental.pallas import tpu as pltpu
from jax.sharding import Mesh, PartitionSpec as P

AXES = {"z1": 4, "z0": 4, "yh": 2, "x": 4, "yl": 2, "core": 2}
DP, FSDP, NEAR = ("z1", "z0", "yh"), ("x", "yl", "core"), ("yl", "core")
CLOSE, FAR = ("yl", "yh", "z0"), ("z1", "yh")
SPLIT = ("x", "core", "yl")


def fake_quantize(factor, bits, scale_exps):
    step = jnp.exp2(-scale_exps.astype(jnp.float32))
    upper = jnp.exp2(bits.astype(jnp.float32) - 1.0)
    ratio = factor / step
    smooth = ratio - jnp.sin(2.0 * math.pi * ratio) / (2.0 * math.pi)
    return step * jnp.clip(smooth, -upper, upper - 1.0)


def flips(n, step):
    return [(j, j ^ step) for j in range(n)]


def exchange(parts, axes):
    return lax.all_to_all(parts, axes, 0, 0, tiled=True)


IN_VMEM = pl.BlockSpec(memory_space=pltpu.VMEM)
IN_SMEM = pl.BlockSpec(memory_space=pltpu.SMEM)
PARAMS = pltpu.CompilerParams(vmem_limit_bytes=40 * 1024 * 1024)


def dot32(a, b, dims=((1,), (0,))):
    return lax.dot_general(a, b, (dims, ((), ())), preferred_element_type=jnp.float32)


def partial_kernel(order_ref, tokens_ref, *refs):
    *piece_refs, out_ref = refs
    n_x, tok, _ = out_ref.shape
    rows = piece_refs[0].shape[0]
    for i in range(n_x):
        total = None
        for k, piece in enumerate(piece_refs):
            start = pl.multiple_of(order_ref[k] * rows, rows)
            term = dot32(tokens_ref[i * tok : (i + 1) * tok, pl.ds(start, rows)], piece[...])
            total = term if total is None else total + term
        out_ref[i] = total


def middle_kernel(scale, parts_ref, target_ref, u_ref, sigma_ref, out_ref):
    n_x, tok, _ = parts_ref.shape
    kvw, rank = u_ref.shape
    out = parts_ref[0]
    for i in range(1, n_x):
        out = out + parts_ref[i]
    sigma = sigma_ref[...]
    u_quant = u_ref[...]
    scaled = (out[:, kvw:] * sigma).astype(jnp.bfloat16)
    residual = out[:, :kvw] + dot32(scaled, u_quant, ((1,), (1,))) - target_ref[...].astype(jnp.float32)
    out_grad = (residual * scale).astype(jnp.bfloat16)
    rank_grad = (dot32(out_grad, u_quant) * sigma).astype(jnp.bfloat16)
    grad_u = dot32(out_grad, scaled, ((0,), (0,)))
    high = grad_u.astype(jnp.bfloat16)
    low = (grad_u - high.astype(jnp.float32)).astype(jnp.bfloat16)
    n_to = out_ref.shape[0]
    each = kvw // n_to
    for i in range(n_to):
        out_ref[i, :tok] = rank_grad
        out_ref[i, tok : tok + each] = high[i * each : (i + 1) * each]
        out_ref[i, tok + each :] = low[i * each : (i + 1) * each]


def grads_kernel(core_ref, tokens_ref, others_ref, arrived_ref, out_ref):
    core = core_ref[0]
    n_from, both, rank = arrived_ref.shape
    n_to, packed, _ = out_ref.shape
    n_x, n_yl = n_from // 2, 2
    rows = others_ref.shape[1] // n_yl
    tok = tokens_ref.shape[0] // n_x
    each = (both - tok) // 2
    per_yl = n_to // n_yl
    v_rows = rows // per_yl
    u_rows = packed - v_rows
    mine = jnp.concatenate([arrived_ref[2 * x + core, :tok] for x in range(n_x)], axis=0)
    other = jnp.concatenate([arrived_ref[2 * x + 1 - core, :tok] for x in range(n_x)], axis=0)
    u_sum = jnp.zeros((each, rank), jnp.float32)
    for i in range(n_from):
        u_sum = u_sum + arrived_ref[i, tok : tok + each].astype(jnp.float32)
        u_sum = u_sum + arrived_ref[i, tok + each :].astype(jnp.float32)
    u_sum = u_sum.astype(jnp.bfloat16)
    repeat = n_to * u_rows // each
    for j in range(n_yl):
        start = pl.multiple_of((2 * j + core) * rows, rows)
        v_part = dot32(tokens_ref[:, pl.ds(start, rows)], mine, ((0,), (0,)))
        v_part = v_part + dot32(others_ref[:, j * rows : (j + 1) * rows], other, ((0,), (0,)))
        v_part = v_part.astype(jnp.bfloat16)
        for r in range(per_yl):
            i = j * per_yl + r
            u_at = i // repeat * u_rows
            out_ref[i, :v_rows] = v_part[r * v_rows : (r + 1) * v_rows]
            out_ref[i, v_rows:] = u_sum[u_at : u_at + u_rows]


def close_sum_kernel(arrived_ref, out_ref):
    total = arrived_ref[0].astype(jnp.float32)
    for i in range(1, arrived_ref.shape[0]):
        total = total + arrived_ref[i].astype(jnp.float32)
    for i in range(out_ref.shape[0]):
        out_ref[i] = total.astype(out_ref.dtype)


def far_v_kernel(arrived_ref, v_ref):
    n_yh = 2
    rows = v_ref.shape[0] // n_yh
    for h in range(n_yh):
        total = arrived_ref[h, :rows].astype(jnp.float32)
        for i in range(h + n_yh, arrived_ref.shape[0], n_yh):
            total = total + arrived_ref[i, :rows].astype(jnp.float32)
        v_ref[h * rows : (h + 1) * rows] = total


def far_u_kernel(arrived_ref, v_ref, u_ref):
    n_yh = 2
    v_rows = v_ref.shape[0] // n_yh
    rows = u_ref.shape[1] // n_yh
    for h in range(n_yh):
        total = arrived_ref[h, v_rows:].astype(jnp.float32)
        for i in range(h + n_yh, arrived_ref.shape[0], n_yh):
            total = total + arrived_ref[i, v_rows:].astype(jnp.float32)
        for i in range(u_ref.shape[0]):
            u_ref[i, h * rows : (h + 1) * rows] = total


def place_kernel(order_ref, u_ref, *refs):
    *piece_refs, v_ref, out_u_ref = refs
    n_yh, n_z0 = 2, order_ref.shape[0]
    half = v_ref.shape[0] // n_yh
    rows = half // n_z0
    pieces = [p[i : i + rows] for p in piece_refs for i in range(0, p.shape[0], rows)]
    for i, piece in enumerate(pieces):
        start = pl.multiple_of(i % n_yh * half + order_ref[i // n_yh] * rows, rows)
        v_ref[pl.ds(start, rows)] = piece
    out_u_ref[...] = u_ref[...]


def kernel_call(kernel, out, name, operands, scalars=0):
    return pl.pallas_call(
        kernel,
        out_shape=out,
        in_specs=[IN_SMEM] * scalars + [IN_VMEM] * (len(operands) - scalars),
        out_specs=jax.tree.map(lambda _: IN_VMEM, out),
        compiler_params=PARAMS,
        name=name,
    )(*operands)


def shards(hidden, target, base_weight, v_factor, u_factor, sigma, bits, v_exps, u_exps):
    n_x, n_z0, n_near = lax.axis_size("x"), lax.axis_size("z0"), lax.axis_size(NEAR)
    tok, _ = hidden.shape
    kvw, rank = u_factor.shape
    rows = v_factor.shape[0]
    me = lax.axis_index(NEAR)
    swap = [(0, 1), (1, 0)]

    v_quant = fake_quantize(v_factor, bits, v_exps).astype(jnp.bfloat16)
    own = jnp.concatenate([base_weight, v_quant], axis=1)
    across = lax.ppermute(own, "yl", swap)
    pieces = [own, lax.ppermute(own, "core", swap), across, lax.ppermute(across, "core", swap)]
    wide = n_near * rows
    columns = lax.all_to_all(hidden.reshape(tok, n_x, wide), "x", 1, 1, tiled=True)
    tokens = columns.transpose(1, 0, 2).reshape(n_x * tok, wide)
    own, u_late = lax.optimization_barrier((own, u_factor))
    u_quant = fake_quantize(u_late, bits, u_exps).astype(jnp.bfloat16)

    f32, bf16 = jnp.float32, jnp.bfloat16
    shape = jax.ShapeDtypeStruct
    order = jnp.bitwise_xor(me, jnp.arange(n_near, dtype=jnp.int32))
    part = kernel_call(
        partial_kernel,
        shape((n_x, tok, kvw + rank), f32),
        "partial_products",
        (order, tokens, *pieces),
        scalars=1,
    )
    core = lax.axis_index("core")
    others = [
        lax.dynamic_slice_in_dim(tokens, (2 * i + 1 - core) * rows, rows, 1)
        for i in range(n_near // 2)
    ]
    others = lax.ppermute(jnp.concatenate(others, axis=1), "core", swap)
    scale = 1.0 / math.sqrt(tok * math.prod(lax.axis_size(a) for a in AXES))
    ranks = kernel_call(
        functools.partial(middle_kernel, scale),
        shape((2 * n_x, tok + kvw // n_x, rank), bf16),
        "residual_and_grad_u",
        (exchange(part, "x"), target, u_quant, sigma.reshape(1, rank)),
    )
    ranks, others = lax.optimization_barrier((ranks, others))
    n_close, n_far = lax.axis_size(CLOSE), lax.axis_size(FAR)
    v_rows, u_rows = wide // (2 * n_close), kvw * n_z0 // (2 * n_x * n_close)
    parts = kernel_call(
        grads_kernel,
        shape((n_close, v_rows + u_rows, rank), bf16),
        "grads_packed",
        (core.reshape(1), tokens, others, exchange(ranks, ("x", "core"))),
        scalars=1,
    )
    mine = kernel_call(
        close_sum_kernel,
        shape((n_far, v_rows + u_rows, rank), bf16),
        "close_sum",
        (exchange(parts, CLOSE),),
    )
    arrived = exchange(mine, FAR)
    v_mine = kernel_call(far_v_kernel, shape((2 * v_rows, rank), f32), "far_v", (arrived,))
    u_mine = kernel_call(
        far_u_kernel,
        shape((lax.axis_size(SPLIT), 2 * u_rows, rank), f32),
        "far_u",
        (arrived, v_mine),
    )
    grad_u = exchange(u_mine, SPLIT).reshape(kvw, rank)
    v_two = jnp.concatenate([v_mine, lax.ppermute(v_mine, "z0", flips(n_z0, 2))], axis=0)
    v_pieces = [v_two, lax.ppermute(v_two, "z0", flips(n_z0, 1))]
    order = jnp.bitwise_xor(lax.axis_index("z0"), jnp.array([0, 2, 1, 3], jnp.int32))
    return kernel_call(
        place_kernel,
        (shape((rows, rank), f32), shape((kvw, rank), f32)),
        "grads",
        (order, grad_u, *v_pieces),
        scalars=1,
    )


def solution(mesh):
    fine = Mesh(mesh.devices.reshape(tuple(AXES.values())), tuple(AXES))
    in_specs = (
        P((*DP, *FSDP), None),
        P((*DP, *FSDP), None),
        P(FSDP, None),
        P(FSDP, None),
        P(),
        P(),
        P(),
        P(),
        P(),
    )
    out_specs = (P(FSDP, None), P())
    return jax.shard_map(shards, mesh=fine, in_specs=in_specs, out_specs=out_specs, check_vma=False)
```

```python
import functools
import math

import jax
import jax.numpy as jnp
from jax import lax
from jax.experimental import pallas as pl
from jax.experimental.pallas import tpu as pltpu
from jax.sharding import Mesh, PartitionSpec as P

AXES = {"z1": 4, "z0": 4, "yh": 2, "x": 4, "yl": 2, "core": 2}
DP, FSDP, NEAR = ("z1", "z0", "yh"), ("x", "yl", "core"), ("yl", "core")
CLOSE, FAR = ("yl", "yh", "z0"), ("z1", "yh")
SPLIT = ("x", "core", "yl")


def fake_quantize(factor, bits, scale_exps):
    step = jnp.exp2(-scale_exps.astype(jnp.float32))
    upper = jnp.exp2(bits.astype(jnp.float32) - 1.0)
    ratio = factor / step
    smooth = ratio - jnp.sin(2.0 * math.pi * ratio) / (2.0 * math.pi)
    return step * jnp.clip(smooth, -upper, upper - 1.0)


def flips(n, step):
    return [(j, j ^ step) for j in range(n)]


def exchange(parts, axes):
    return lax.all_to_all(parts, axes, 0, 0, tiled=True)


IN_VMEM = pl.BlockSpec(memory_space=pltpu.VMEM)
IN_SMEM = pl.BlockSpec(memory_space=pltpu.SMEM)
PARAMS = pltpu.CompilerParams(vmem_limit_bytes=40 * 1024 * 1024)


def dot32(a, b, dims=((1,), (0,))):
    return lax.dot_general(a, b, (dims, ((), ())), preferred_element_type=jnp.float32)


def partial_kernel(order_ref, tokens_ref, *refs):
    *piece_refs, out_ref = refs
    n_x, tok, _ = out_ref.shape
    rows = piece_refs[0].shape[0]
    for i in range(n_x):
        total = None
        for k, piece in enumerate(piece_refs):
            start = pl.multiple_of(order_ref[k] * rows, rows)
            term = dot32(tokens_ref[i * tok : (i + 1) * tok, pl.ds(start, rows)], piece[...])
            total = term if total is None else total + term
        out_ref[i] = total


def middle_kernel(scale, parts_ref, target_ref, u_ref, sigma_ref, out_ref):
    n_x, tok, _ = parts_ref.shape
    kvw, rank = u_ref.shape
    out = parts_ref[0]
    for i in range(1, n_x):
        out = out + parts_ref[i]
    sigma = sigma_ref[...]
    u_quant = u_ref[...]
    scaled = (out[:, kvw:] * sigma).astype(jnp.bfloat16)
    residual = out[:, :kvw] + dot32(scaled, u_quant, ((1,), (1,))) - target_ref[...].astype(jnp.float32)
    out_grad = (residual * scale).astype(jnp.bfloat16)
    rank_grad = (dot32(out_grad, u_quant) * sigma).astype(jnp.bfloat16)
    grad_u = dot32(out_grad, scaled, ((0,), (0,)))
    high = grad_u.astype(jnp.bfloat16)
    low = (grad_u - high.astype(jnp.float32)).astype(jnp.bfloat16)
    n_to = out_ref.shape[0]
    each = kvw // n_to
    for i in range(n_to):
        out_ref[i, :tok] = rank_grad
        out_ref[i, tok : tok + each] = high[i * each : (i + 1) * each]
        out_ref[i, tok + each :] = low[i * each : (i + 1) * each]


def grads_kernel(core_ref, tokens_ref, others_ref, arrived_ref, out_ref):
    core = core_ref[0]
    n_from, both, rank = arrived_ref.shape
    n_to, packed, _ = out_ref.shape
    n_x, n_yl = n_from // 2, 2
    rows = others_ref.shape[1] // n_yl
    tok = tokens_ref.shape[0] // n_x
    each = (both - tok) // 2
    per_yl = n_to // n_yl
    v_rows = rows // per_yl
    u_rows = packed - v_rows
    mine = jnp.concatenate([arrived_ref[2 * x + core, :tok] for x in range(n_x)], axis=0)
    other = jnp.concatenate([arrived_ref[2 * x + 1 - core, :tok] for x in range(n_x)], axis=0)
    u_sum = jnp.zeros((each, rank), jnp.float32)
    for i in range(n_from):
        u_sum = u_sum + arrived_ref[i, tok : tok + each].astype(jnp.float32)
        u_sum = u_sum + arrived_ref[i, tok + each :].astype(jnp.float32)
    u_sum = u_sum.astype(jnp.bfloat16)
    repeat = n_to * u_rows // each
    for j in range(n_yl):
        start = pl.multiple_of((2 * j + core) * rows, rows)
        v_part = dot32(tokens_ref[:, pl.ds(start, rows)], mine, ((0,), (0,)))
        v_part = v_part + dot32(others_ref[:, j * rows : (j + 1) * rows], other, ((0,), (0,)))
        v_part = v_part.astype(jnp.bfloat16)
        for r in range(per_yl):
            i = j * per_yl + r
            u_at = i // repeat * u_rows
            out_ref[i, :v_rows] = v_part[r * v_rows : (r + 1) * v_rows]
            out_ref[i, v_rows:] = u_sum[u_at : u_at + u_rows]


def close_sum_kernel(arrived_ref, out_ref):
    total = arrived_ref[0].astype(jnp.float32)
    for i in range(1, arrived_ref.shape[0]):
        total = total + arrived_ref[i].astype(jnp.float32)
    for i in range(out_ref.shape[0]):
        out_ref[i] = total.astype(out_ref.dtype)


def far_v_kernel(arrived_ref, v_ref):
    n_yh = 2
    rows = v_ref.shape[0] // n_yh
    for h in range(n_yh):
        total = arrived_ref[h, :rows].astype(jnp.float32)
        for i in range(h + n_yh, arrived_ref.shape[0], n_yh):
            total = total + arrived_ref[i, :rows].astype(jnp.float32)
        v_ref[h * rows : (h + 1) * rows] = total


def far_u_kernel(arrived_ref, v_ref, u_ref):
    n_yh = 2
    v_rows = v_ref.shape[0] // n_yh
    rows = u_ref.shape[1] // n_yh
    for h in range(n_yh):
        total = arrived_ref[h, v_rows:].astype(jnp.float32)
        for i in range(h + n_yh, arrived_ref.shape[0], n_yh):
            total = total + arrived_ref[i, v_rows:].astype(jnp.float32)
        for i in range(u_ref.shape[0]):
            u_ref[i, h * rows : (h + 1) * rows] = total


def place_kernel(order_ref, u_ref, *refs):
    *piece_refs, v_ref, out_u_ref = refs
    n_yh, n_z0 = 2, order_ref.shape[0]
    half = v_ref.shape[0] // n_yh
    rows = half // n_z0
    pieces = [p[i : i + rows] for p in piece_refs for i in range(0, p.shape[0], rows)]
    for i, piece in enumerate(pieces):
        start = pl.multiple_of(i % n_yh * half + order_ref[i // n_yh] * rows, rows)
        v_ref[pl.ds(start, rows)] = piece
    out_u_ref[...] = u_ref[...]


def kernel_call(kernel, out, name, operands, scalars=0):
    return pl.pallas_call(
        kernel,
        out_shape=out,
        in_specs=[IN_SMEM] * scalars + [IN_VMEM] * (len(operands) - scalars),
        out_specs=jax.tree.map(lambda _: IN_VMEM, out),
        compiler_params=PARAMS,
        name=name,
    )(*operands)


def shards(hidden, target, base_weight, v_factor, u_factor, sigma, bits, v_exps, u_exps):
    n_x, n_z0, n_near = lax.axis_size("x"), lax.axis_size("z0"), lax.axis_size(NEAR)
    tok, _ = hidden.shape
    kvw, rank = u_factor.shape
    rows = v_factor.shape[0]
    me = lax.axis_index(NEAR)
    swap = [(0, 1), (1, 0)]

    v_quant = fake_quantize(v_factor, bits, v_exps).astype(jnp.bfloat16)
    own = jnp.concatenate([base_weight, v_quant], axis=1)
    across = lax.ppermute(own, "yl", swap)
    pieces = [own, lax.ppermute(own, "core", swap), across, lax.ppermute(across, "core", swap)]
    wide = n_near * rows
    columns = lax.all_to_all(hidden.reshape(tok, n_x, wide), "x", 1, 1, tiled=True)
    tokens = columns.transpose(1, 0, 2).reshape(n_x * tok, wide)
    own, u_late = lax.optimization_barrier((own, u_factor))
    u_quant = fake_quantize(u_late, bits, u_exps).astype(jnp.bfloat16)

    f32, bf16 = jnp.float32, jnp.bfloat16
    shape = jax.ShapeDtypeStruct
    order = jnp.bitwise_xor(me, jnp.arange(n_near, dtype=jnp.int32))
    order, u_quant = lax.optimization_barrier((order, u_quant))
    part = kernel_call(
        partial_kernel,
        shape((n_x, tok, kvw + rank), f32),
        "partial_products",
        (order, tokens, *pieces),
        scalars=1,
    )
    core = lax.axis_index("core")
    others = [
        lax.dynamic_slice_in_dim(tokens, (2 * i + 1 - core) * rows, rows, 1)
        for i in range(n_near // 2)
    ]
    others = lax.ppermute(jnp.concatenate(others, axis=1), "core", swap)
    scale = 1.0 / math.sqrt(tok * math.prod(lax.axis_size(a) for a in AXES))
    ranks = kernel_call(
        functools.partial(middle_kernel, scale),
        shape((2 * n_x, tok + kvw // n_x, rank), bf16),
        "residual_and_grad_u",
        (exchange(part, "x"), target, u_quant, sigma.reshape(1, rank)),
    )
    ranks, others = lax.optimization_barrier((ranks, others))
    n_close, n_far = lax.axis_size(CLOSE), lax.axis_size(FAR)
    v_rows, u_rows = wide // (2 * n_close), kvw * n_z0 // (2 * n_x * n_close)
    parts = kernel_call(
        grads_kernel,
        shape((n_close, v_rows + u_rows, rank), bf16),
        "grads_packed",
        (core.reshape(1), tokens, others, exchange(ranks, ("x", "core"))),
        scalars=1,
    )
    mine = kernel_call(
        close_sum_kernel,
        shape((n_far, v_rows + u_rows, rank), bf16),
        "close_sum",
        (exchange(parts, CLOSE),),
    )
    arrived = exchange(mine, FAR)
    v_mine = kernel_call(far_v_kernel, shape((2 * v_rows, rank), f32), "far_v", (arrived,))
    u_mine = kernel_call(
        far_u_kernel,
        shape((lax.axis_size(SPLIT), 2 * u_rows, rank), f32),
        "far_u",
        (arrived, v_mine),
    )
    grad_u = exchange(u_mine, SPLIT).reshape(kvw, rank)
    v_two = jnp.concatenate([v_mine, lax.ppermute(v_mine, "z0", flips(n_z0, 2))], axis=0)
    v_pieces = [v_two, lax.ppermute(v_two, "z0", flips(n_z0, 1))]
    order = jnp.bitwise_xor(lax.axis_index("z0"), jnp.array([0, 2, 1, 3], jnp.int32))
    return kernel_call(
        place_kernel,
        (shape((rows, rank), f32), shape((kvw, rank), f32)),
        "grads",
        (order, grad_u, *v_pieces),
        scalars=1,
    )


def solution(mesh):
    fine = Mesh(mesh.devices.reshape(tuple(AXES.values())), tuple(AXES))
    in_specs = (
        P((*DP, *FSDP), None),
        P((*DP, *FSDP), None),
        P(FSDP, None),
        P(FSDP, None),
        P(),
        P(),
        P(),
        P(),
        P(),
    )
    out_specs = (P(FSDP, None), P())
    return jax.shard_map(shards, mesh=fine, in_specs=in_specs, out_specs=out_specs, check_vma=False)
```
